32 devices in a mesh: groups: 2 (over y), expert: 4 (over z), head: 4 (over x, core).
Axes of the slice: x: 2, y: 2, z: 4, core: 2. Of those that a mesh axis runs over, the one named last changes fastest.
Arguments:
- residual: bfloat16 [64, 3584], P(('groups', 'expert')), parts along dimension 0, may hold values from -6 to 6
- query_latent: bfloat16 [64, 32, 512], P(('groups', 'expert'), 'head'), parts along dimension 0, may hold values from -16 to 16
- query_rope: bfloat16 [64, 32, 64], P(('groups', 'expert'), 'head'), parts along dimension 0, may hold values from -5 to 5
- cache_latent: bfloat16 [64, 32, 512], P(('groups', 'expert')), parts along dimension 0, may hold values from -4 to 4
- cache_rope: bfloat16 [64, 32, 64], P(('groups', 'expert')), parts along dimension 0, may hold values from -5 to 5
- absorb_value: bfloat16 [32, 512, 128], P('head'), may hold values from -0.25 to 0.25
- out_proj: bfloat16 [4096, 3584], P('head', 'expert'), may hold values from -0.09375 to 0.09375
- norm_gain: float32 [3584], replicated, may hold values from 0.5 to 1.5
- routes: int32 [64, 8], P(('groups', 'expert')), parts along dimension 0, may hold values from 0 to 31, all different within a row; in each aligned block of 4 rows (0 to 3, 4 to 7, ...) at most 2 rows name the same one
- route_weights: float32 [64, 8], P(('groups', 'expert')), parts along dimension 0, may hold values from 0.1 to 1
- w_gate: bfloat16 [32, 3584, 1024], P('expert', None, 'head'), may hold values from -0.09375 to 0.09375
- w_up: bfloat16 [32, 3584, 1024], P('expert', None, 'head'), may hold values from -0.09375 to 0.09375
- w_down: bfloat16 [32, 1024, 3584], P('expert', 'head'), may hold values from -0.1875 to 0.1875
Outputs:
- mid_state: bfloat16 [64, 3584], P(('groups', 'expert')), parts along dimension 0
- mixed: bfloat16 [64, 3584], P(('groups', 'expert')), parts along dimension 0
The draws below stay inside these ranges and needn't reach their ends.
There are 2 independent parts, one for each index of `groups`. The reference program is written for one: setup_inputs(seed, part) draws one part's arguments, and reference() takes and returns one part's arrays. A program takes and returns all parts, laid end to end along the dimension named above; an argument that names none is the same for every part. Nothing has to cross between parts.
Inputs may be any that keep to these rules, and one draw needn't show every extreme that they name: `routes`: each row names 8 different experts. In each aligned block of 4 rows (the rows of one micro-batch of one index of expert) no expert is named by more than 2 rows, a bound that some block reaches.
All inputs are finite; a program needn't handle non-finite values.
Results may differ from the reference program's by a relative error of at most 0.012.
Values may be sent and summed in bfloat16 or wider, within the bound.
No kernel may reach another device: no remote copies, remote signals or barrier semaphores. Data moves between devices by JAX's collectives and lax.ppermute only.
A program may use at most 192 MiB of HBM per device.

```python
import math
import jax
import jax.numpy as jnp
import numpy as np
from jax import lax

D = 3584
FF = 1024
LATENT = 512
ROPE = 64
VDIM = 128
EXPERTS = 32
TOP = 8
MB = 4
CTX = 32
CAP = 2
HEADS = 32
TOKENS = 32


def shared_normal(key):
    return jnp.clip(jax.random.normal(key, (TOKENS, CTX, LATENT), jnp.float32), -4.0, 4.0)


def draw_cache_latent(key, part):
    base_latent = shared_normal(key)
    return base_latent.astype(jnp.bfloat16)


def draw_query_latent(key, part):
    key = jax.random.fold_in(key, 12)
    own_query = jnp.clip(jax.random.normal(key, (TOKENS, HEADS, LATENT), jnp.float32), -4.0, 4.0)
    return own_query.astype(jnp.bfloat16)


def levels(own_key, dims, split, low, top_value):
    def one(dim, shards_of):
        steps = jax.random.uniform(jax.random.fold_in(jax.random.fold_in(own_key, 6), dim), (shards_of,), jnp.float32, low / len(split), top_value / len(split))
        return jnp.repeat(jnp.exp(steps), dims[dim] // shards_of).reshape((-1,) + (1,) * (len(dims) - dim - 1))

    loudness = one(*split[0])
    for cut in split[1:]:
        loudness = loudness * one(*cut)
    return loudness


def assign_block(rng, own, number, rows, count, top, bound, lean):
    order = jax.random.permutation(rng, count)
    packed, usual = shares(count, rows * top, bound, lean, True), shares(count, rows * top, bound, lean, False)
    places = jnp.arange(count)

    def named(tallies, offset_by):
        used = int((tallies > 0).sum())
        fixed = max(1, used // 4)
        shifted = fixed + (places - fixed + offset_by * (used - fixed)) % max(1, count - fixed)
        return jnp.zeros((count,), jnp.int32).at[order[jnp.where(places < fixed, places, shifted)]].set(jnp.asarray(tallies, jnp.int32))

    tallies = jnp.where(number % 4 == 0, named(packed, number // 4), named(usual, number - number // 4 - 1))
    mixed = jax.random.permutation(jax.random.fold_in(own, 3), count)
    giver, receiver = mixed[0:count // 2 * 2:2], mixed[1:count // 2 * 2:2]
    margin = jnp.minimum(tallies[giver] - 1, bound - tallies[receiver]) // 2
    margin = jnp.where((giver == order[0]) | (receiver == order[0]) | (tallies[receiver] == 0), 0, jnp.maximum(margin, 0))
    shifted = jax.random.randint(jax.random.fold_in(own, 4), (count // 2,), 0, 1 << 20) % (margin + 1)
    tallies = tallies.at[giver].add(-shifted).at[receiver].add(shifted)
    members = jnp.searchsorted(jnp.cumsum(tallies), jnp.arange(rows * top), side="right").astype(jnp.int32)
    listing = members.reshape(top, rows).T
    listing = listing[jax.random.permutation(jax.random.fold_in(own, 1), rows)]
    offset_by = jax.random.randint(jax.random.fold_in(own, 2), (rows, 1), 0, top)
    return jnp.take_along_axis(listing, (jnp.arange(top)[None, :] + offset_by) % top, axis=1)


def shares(number_of, total, bound, lean, full):
    weights = [(1 << 20) // math.isqrt(standing ** lean) + 1 for standing in range(1, number_of + 1)]
    largest = bound if full else min(bound, max(-(-total // number_of), total * weights[0] // sum(weights)))
    least = 1 if total - largest >= number_of - 1 else 0
    given, spare = [largest] + [least] * (number_of - 1), total - largest - least * (number_of - 1)
    while spare > 0:
        candidates = [i for i in range(1, number_of) if given[i] < largest] or [i for i in range(1, number_of) if given[i] < bound]
        mass, left = sum([weights[i] for i in candidates]), spare
        for i in candidates:
            extra = min(bound - given[i], max(1, left * weights[i] // mass), spare)
            given[i] = given[i] + extra
            spare = spare - extra
    return np.array(given)


def normal_values(key, shape, spread, limit, cuts=(), held_as=jnp.bfloat16):
    gain = levels(key, shape, cuts, -0.22, 0.18) if cuts else 1.0
    entries = jax.random.normal(key, shape, jnp.float32) * spread * gain
    return jnp.minimum(jnp.maximum(entries, -limit), limit).astype(held_as)


def setup_inputs(seed: int = 0, part: int = 0) -> dict:
    key_of = jax.random.split(jax.random.key(seed), 14)
    part_splits = jax.random.split(jax.random.fold_in(key_of[13], part), 14)
    residual = normal_values(part_splits[0], (TOKENS, D), 1.0, 6.0, ((0, 4),))
    query_latent = draw_query_latent(jax.random.fold_in(jax.random.fold_in(key_of[13], part), 71), part)
    query_rope = normal_values(part_splits[2], (TOKENS, HEADS, ROPE), 1.0, 5.0, ((0, 4), (1, 4)))
    cache_latent = draw_cache_latent(jax.random.fold_in(jax.random.fold_in(key_of[13], part), 71), part)
    cache_rope = normal_values(part_splits[4], (TOKENS, CTX, ROPE), 1.0, 5.0, ((0, 4),))
    absorb_value = normal_values(key_of[5], (HEADS, LATENT, VDIM), LATENT ** -0.5, 0.25, ((0, 4),))
    out_proj = normal_values(key_of[6], (HEADS * VDIM, D), (HEADS * VDIM) ** -0.5, 0.09375, ((0, 4), (1, 4)))
    norm_gain = jnp.clip(1.0 + 0.1 * jax.random.normal(key_of[7], (D,), jnp.float32), 0.5, 1.5)
    routes_keys = jax.random.split(jax.random.fold_in(part_splits[8], 1), TOKENS // MB)
    routes_turns = jax.random.permutation(jax.random.fold_in(part_splits[8], 3), TOKENS // MB)
    routes = jax.vmap(lambda own, number: assign_block(jax.random.fold_in(part_splits[8], 2), own, number, MB, EXPERTS, TOP, CAP, 2))(routes_keys, routes_turns).reshape((TOKENS, TOP))
    route_weights = jnp.clip(jnp.exp(math.log(1.0) - 2.3025851 * jax.random.uniform(part_splits[9], (TOKENS, TOP), jnp.float32) ** levels(part_splits[9], (TOKENS, TOP), ((0, 4),), -0.2, 0.2)), 0.1, 1.0)
    w_gate = normal_values(key_of[10], (EXPERTS, D, FF), D ** -0.5, 0.09375, ((0, 4), (2, 4)))
    w_up = normal_values(key_of[11], (EXPERTS, D, FF), D ** -0.5, 0.09375, ((0, 4), (2, 4)))
    w_down = normal_values(key_of[12], (EXPERTS, FF, D), FF ** -0.5, 0.1875, ((0, 4), (1, 4)))
    return dict(residual=residual, query_latent=query_latent, query_rope=query_rope, cache_latent=cache_latent, cache_rope=cache_rope, absorb_value=absorb_value, out_proj=out_proj, norm_gain=norm_gain, routes=routes, route_weights=route_weights, w_gate=w_gate, w_up=w_up, w_down=w_down)


def reference(residual, query_latent, query_rope, cache_latent, cache_rope, absorb_value, out_proj, norm_gain, routes, route_weights, w_gate, w_up, w_down):
    highest = lax.Precision.HIGHEST
    score_scale = (VDIM + ROPE) ** (-0.5)
    scores = jnp.einsum('thl,tcl->thc', query_latent.astype(jnp.float32), cache_latent.astype(jnp.float32), precision=highest)
    scores = scores + jnp.einsum('thr,tcr->thc', query_rope.astype(jnp.float32), cache_rope.astype(jnp.float32), precision=highest)
    scores = scores * score_scale
    probs = jax.nn.softmax(scores, axis=-1).astype(jnp.bfloat16)
    head_latent = jnp.einsum('thc,tcl->thl', probs.astype(jnp.float32), cache_latent.astype(jnp.float32), precision=highest).astype(jnp.bfloat16)
    head_out = jnp.einsum('thl,hlv->thv', head_latent.astype(jnp.float32), absorb_value.astype(jnp.float32), precision=highest).astype(jnp.bfloat16)
    head_out = head_out.reshape(TOKENS, HEADS * VDIM)
    attention = jnp.dot(head_out, out_proj, preferred_element_type=jnp.float32).astype(jnp.bfloat16)
    mid_state = (residual.astype(jnp.float32) + attention.astype(jnp.float32)).astype(jnp.bfloat16)
    mid_float = mid_state.astype(jnp.float32)
    normed = (mid_float * lax.rsqrt(lax.optimization_barrier(jnp.mean(mid_float * mid_float, axis=-1, keepdims=True)) + 1e-06) * norm_gain).astype(jnp.bfloat16)
    block_count = TOKENS // MB
    block_ids = routes.reshape(block_count, MB * TOP)
    onehot = (block_ids[:, :, None] == jnp.arange(EXPERTS, dtype=jnp.int32)[None, None, :]).astype(jnp.int32)
    before = jnp.cumsum(onehot, axis=1) - onehot
    slot_rank = lax.optimization_barrier(jnp.sum(before * onehot, axis=-1))
    position = (jnp.arange(block_count, dtype=jnp.int32)[:, None] * CAP + slot_rank).reshape(-1).astype(jnp.int32)
    expert_ids = routes.reshape(-1).astype(jnp.int32)
    token_ids = jnp.repeat(jnp.arange(TOKENS, dtype=jnp.int32), TOP)
    slot_table = jnp.full((EXPERTS, block_count * CAP), TOKENS, jnp.int32).at[expert_ids, position].set(token_ids)
    padded = jnp.concatenate([normed, jnp.zeros((1, D), normed.dtype)], axis=0)
    gathered = padded[slot_table]

    def run_expert(operands):
        rows_in, gate_weight, up_weight, down_weight = operands
        gate_act = jnp.dot(rows_in, gate_weight, preferred_element_type=jnp.float32)
        up_act = jnp.dot(rows_in, up_weight, preferred_element_type=jnp.float32)
        hidden = (jax.nn.silu(gate_act) * up_act).astype(jnp.bfloat16)
        return jnp.dot(hidden, down_weight, preferred_element_type=jnp.float32).astype(jnp.bfloat16)
    expert_out = lax.map(run_expert, (gathered, w_gate, w_up, w_down))
    picked = expert_out[expert_ids, position].reshape(TOKENS, TOP, D).astype(jnp.float32)
    mixed = lax.optimization_barrier(jnp.sum(picked * route_weights[:, :, None], axis=1)).astype(jnp.bfloat16)
    return (mid_state, mixed)
```

```python
import jax
import jax.numpy as jnp
from jax import lax
from jax.sharding import PartitionSpec as P


def swap(x, axis, size, step):
    return lax.ppermute(x, axis, [(s, s ^ step) for s in range(size)])


def gather_rows(x, axis):
    size = lax.axis_size(axis)
    me = lax.axis_index(axis)
    out = jnp.zeros((size,) + x.shape, x.dtype)
    out = lax.dynamic_update_index_in_dim(out, x, me, 0)
    for step in range(1, size):
        out = lax.dynamic_update_index_in_dim(out, swap(x, axis, size, step), me ^ step, 0)
    return out


def scatter_sum(blocks, axis):
    size = lax.axis_size(axis)
    me = lax.axis_index(axis)
    total = lax.dynamic_index_in_dim(blocks, me, 0, keepdims=False)
    for step in range(1, size):
        block = lax.dynamic_index_in_dim(blocks, me ^ step, 0, keepdims=False)
        total = total + swap(block.astype(jnp.bfloat16), axis, size, step).astype(jnp.float32)
    return total


def sum_all(x, axis):
    size = lax.axis_size(axis)
    step = 1
    while step < size:
        x = x + swap(x.astype(jnp.bfloat16), axis, size, step).astype(jnp.float32)
        step *= 2
    return x


def attend(query_lat, query_rot, cache_lat, cache_rot, absorb_value, score_scale):
    scores = jnp.einsum("thl,tcl->thc", query_lat, cache_lat, preferred_element_type=jnp.float32)
    scores = scores + jnp.einsum(
        "thr,tcr->thc", query_rot, cache_rot, preferred_element_type=jnp.float32
    )
    probs = jax.nn.softmax(scores * score_scale, axis=-1).astype(jnp.bfloat16)
    latent = jnp.einsum(
        "thc,tcl->thl", probs, cache_lat, preferred_element_type=jnp.float32
    ).astype(jnp.bfloat16)
    per_head = jnp.einsum(
        "thl,hlv->thv", latent, absorb_value, preferred_element_type=jnp.float32
    ).astype(jnp.bfloat16)
    return per_head.reshape(per_head.shape[0], per_head.shape[1] * per_head.shape[2])


def shards(
    residual,
    query_latent,
    query_rope,
    cache_latent,
    cache_rope,
    absorb_value,
    out_proj,
    norm_gain,
    routes,
    route_weights,
    w_gate,
    w_up,
    w_down,
):
    sources = lax.axis_size("expert")
    me = lax.axis_index("expert")
    experts, model_d, hidden_f = w_gate.shape
    rows = residual.shape[0]
    tokens = rows * sources
    score_scale = (absorb_value.shape[2] + query_rope.shape[2]) ** (-0.5)
    all_res = gather_rows(residual, "expert").reshape(tokens, model_d)
    all_routes = gather_rows(routes, "expert").reshape(tokens, -1)
    all_weights = gather_rows(route_weights, "expert").reshape(tokens, -1)
    own_ids = me * experts + jnp.arange(experts, dtype=jnp.int32)
    named = all_routes[:, None, :] == own_ids[None, :, None]
    chosen = jnp.any(named, axis=2)
    weight = jnp.sum(jnp.where(named, all_weights[:, None, :], 0.0), axis=2)

    per_head = attend(
        query_latent, query_rope, cache_latent, cache_rope, absorb_value, score_scale
    )
    all_heads = gather_rows(per_head, "expert").reshape(tokens, -1)
    partial = jnp.dot(all_heads, out_proj, preferred_element_type=jnp.float32)
    summed = sum_all(partial, "head").astype(jnp.bfloat16)
    attention = gather_rows(summed, "expert")
    attention = attention.transpose(1, 0, 2).reshape(tokens, model_d)
    mid = (all_res.astype(jnp.float32) + attention.astype(jnp.float32)).astype(jnp.bfloat16)
    mid_float = mid.astype(jnp.float32)
    normed = (
        mid_float
        * lax.rsqrt(jnp.mean(mid_float * mid_float, axis=-1, keepdims=True) + 1e-06)
        * norm_gain
    ).astype(jnp.bfloat16)
    gate = jnp.einsum("td,edf->etf", normed, w_gate, preferred_element_type=jnp.float32)
    up = jnp.einsum("td,edf->etf", normed, w_up, preferred_element_type=jnp.float32)
    hidden = jnp.where(
        chosen.T[:, :, None], jax.nn.silu(gate) * up * weight.T[:, :, None], 0.0
    ).astype(jnp.bfloat16)
    down = jnp.einsum("etf,efd->td", hidden, w_down, preferred_element_type=jnp.float32)
    mixed = scatter_sum(down.reshape(sources, rows, model_d), "expert")
    mixed = sum_all(mixed, "head").astype(jnp.bfloat16)
    own_mid = lax.dynamic_slice_in_dim(mid, me * rows, rows, 0)
    return own_mid, mixed


def solution(mesh):
    in_specs = (
        P(("groups", "expert"), None),
        P(("groups", "expert"), "head", None),
        P(("groups", "expert"), "head", None),
        P(("groups", "expert"), None, None),
        P(("groups", "expert"), None, None),
        P("head", None, None),
        P("head", "expert"),
        P(),
        P(("groups", "expert"), None),
        P(("groups", "expert"), None),
        P("expert", None, "head"),
        P("expert", None, "head"),
        P("expert", "head", None),
    )
    out_specs = (P(("groups", "expert"), None), P(("groups", "expert"), None))
    return jax.shard_map(shards, mesh=mesh, in_specs=in_specs, out_specs=out_specs, check_vma=False)
```

```python
import functools

import jax
import jax.numpy as jnp
from jax import lax
from jax.experimental import pallas as pl
from jax.experimental.pallas import tpu as pltpu
from jax.sharding import PartitionSpec as P

LANES = 128
ROWS = 8
VMEM = pl.BlockSpec(memory_space=pltpu.VMEM)
SMEM = pl.BlockSpec(memory_space=pltpu.SMEM)
FLOPS = (2 * 10**10, 2 * 10**10, 2 * 10**10, 2 * 10**10, 10**10)


def swap(x, axis, size, step):
    return lax.ppermute(x, axis, [(s, s ^ step) for s in range(size)])


def gather_rows(x, axis):
    size = lax.axis_size(axis)
    me = lax.axis_index(axis)
    out = jnp.zeros((size,) + x.shape, x.dtype)
    out = lax.dynamic_update_index_in_dim(out, x, me, 0)
    for step in range(1, size):
        out = lax.dynamic_update_index_in_dim(out, swap(x, axis, size, step), me ^ step, 0)
    return out


def scatter_sum(blocks, axis):
    size = lax.axis_size(axis)
    me = lax.axis_index(axis)
    total = lax.dynamic_index_in_dim(blocks, me, 0, keepdims=False)
    for step in range(1, size):
        block = lax.dynamic_index_in_dim(blocks, me ^ step, 0, keepdims=False)
        total = total + swap(block.astype(jnp.bfloat16), axis, size, step).astype(jnp.float32)
    return total


def sum_all(x, axis):
    size = lax.axis_size(axis)
    step = 1
    while step < size:
        x = x + swap(x.astype(jnp.bfloat16), axis, size, step).astype(jnp.float32)
        step *= 2
    return x


def attend(query_lat, query_rot, cache_lat, cache_rot, absorb_value, score_scale):
    scores = jnp.einsum("thl,tcl->thc", query_lat, cache_lat, preferred_element_type=jnp.float32)
    scores = scores + jnp.einsum(
        "thr,tcr->thc", query_rot, cache_rot, preferred_element_type=jnp.float32
    )
    probs = jax.nn.softmax(scores * score_scale, axis=-1).astype(jnp.bfloat16)
    latent = jnp.einsum(
        "thc,tcl->thl", probs, cache_lat, preferred_element_type=jnp.float32
    ).astype(jnp.bfloat16)
    per_head = jnp.einsum(
        "thl,hlv->thv", latent, absorb_value, preferred_element_type=jnp.float32
    ).astype(jnp.bfloat16)
    return per_head.reshape(per_head.shape[0], per_head.shape[1] * per_head.shape[2])


def plain_shards(
    residual,
    query_latent,
    query_rope,
    cache_latent,
    cache_rope,
    absorb_value,
    out_proj,
    norm_gain,
    routes,
    route_weights,
    w_gate,
    w_up,
    w_down,
):
    sources = lax.axis_size("expert")
    me = lax.axis_index("expert")
    experts, model_d, hidden_f = w_gate.shape
    rows = residual.shape[0]
    tokens = rows * sources
    score_scale = (absorb_value.shape[2] + query_rope.shape[2]) ** (-0.5)
    all_res = gather_rows(residual, "expert").reshape(tokens, model_d)
    all_routes = gather_rows(routes, "expert").reshape(tokens, -1)
    all_weights = gather_rows(route_weights, "expert").reshape(tokens, -1)
    own_ids = me * experts + jnp.arange(experts, dtype=jnp.int32)
    named = all_routes[:, None, :] == own_ids[None, :, None]
    chosen = jnp.any(named, axis=2)
    weight = jnp.sum(jnp.where(named, all_weights[:, None, :], 0.0), axis=2)

    per_head = attend(
        query_latent, query_rope, cache_latent, cache_rope, absorb_value, score_scale
    )
    all_heads = gather_rows(per_head, "expert").reshape(tokens, -1)
    partial = jnp.dot(all_heads, out_proj, preferred_element_type=jnp.float32)
    summed = sum_all(partial, "head").astype(jnp.bfloat16)
    attention = gather_rows(summed, "expert")
    attention = attention.transpose(1, 0, 2).reshape(tokens, model_d)
    mid = (all_res.astype(jnp.float32) + attention.astype(jnp.float32)).astype(jnp.bfloat16)
    mid_float = mid.astype(jnp.float32)
    normed = (
        mid_float
        * lax.rsqrt(jnp.mean(mid_float * mid_float, axis=-1, keepdims=True) + 1e-06)
        * norm_gain
    ).astype(jnp.bfloat16)
    gate = jnp.einsum("td,edf->etf", normed, w_gate, preferred_element_type=jnp.float32)
    up = jnp.einsum("td,edf->etf", normed, w_up, preferred_element_type=jnp.float32)
    hidden = jnp.where(
        chosen.T[:, :, None], jax.nn.silu(gate) * up * weight.T[:, :, None], 0.0
    ).astype(jnp.bfloat16)
    down = jnp.einsum("etf,efd->td", hidden, w_down, preferred_element_type=jnp.float32)
    mixed = scatter_sum(down.reshape(sources, rows, model_d), "expert")
    mixed = sum_all(mixed, "head").astype(jnp.bfloat16)
    own_mid = lax.dynamic_slice_in_dim(mid, me * rows, rows, 0)
    return own_mid, mixed


def call(body, outs, *args, limit, scratch=(), flops=None, specs=None):
    estimate = None
    if flops is not None:
        estimate = pl.CostEstimate(flops=flops, bytes_accessed=1 << 20, transcendentals=0)
    return pl.pallas_call(
        body,
        out_shape=outs,
        in_specs=[VMEM] * len(args) if specs is None else specs,
        out_specs=jax.tree.map(lambda _: VMEM, outs),
        scratch_shapes=list(scratch),
        compiler_params=pltpu.CompilerParams(vmem_limit_bytes=limit),
        cost_estimate=estimate,
    )(*args)


def bf16(*shape):
    return jax.ShapeDtypeStruct(shape, jnp.bfloat16)


def f32(*shape):
    return jax.ShapeDtypeStruct(shape, jnp.float32)


def dot(a, b):
    return jnp.dot(a, b, preferred_element_type=jnp.float32)


def dot_t(a, b):
    return lax.dot_general(a, b, (((1,), (1,)), ((), ())), preferred_element_type=jnp.float32)


def rows_of(x, first, second):
    return x.astype(jnp.float32).reshape(first * second, x.shape[2]).astype(x.dtype)


def attend_kernel(scale, *refs):
    sources, (heads_ref, res_out_ref, table_ref), held, sems = refs[:8], refs[8:11], refs[11:19], refs[19]
    copies = [
        pltpu.make_async_copy(source, place, sems.at[i])
        for i, (source, place) in enumerate(zip(sources, held))
    ]
    for copy in copies:
        copy.start()
    ql_ref, cl_ref, qr_ref, cr_ref, av_ref, res_ref, routes_ref, weights_ref = held
    t, h, _ = ql_ref.shape
    c = cl_ref.shape[1]
    vdim = av_ref.shape[2]
    for copy in copies[:4]:
        copy.wait()
    cache = rows_of(cl_ref[...], t, c)
    scores = dot_t(rows_of(ql_ref[...], t, h), cache)
    scores = scores + dot_t(rows_of(qr_ref[...], t, h), rows_of(cr_ref[...], t, c))
    row_t = lax.broadcasted_iota(jnp.int32, (t * h, t * c), 0) // h
    col_t = lax.broadcasted_iota(jnp.int32, (t * h, t * c), 1) // c
    scores = jnp.where(row_t == col_t, scores * scale, -jnp.inf)
    top = jnp.max(scores, axis=-1, keepdims=True)
    exps = jnp.exp(scores - top)
    probs = (exps / jnp.sum(exps, axis=-1, keepdims=True)).astype(jnp.bfloat16)
    latent = dot(probs, cache).astype(jnp.bfloat16)
    to_row = lax.broadcasted_iota(jnp.int32, (t * h, t * h), 0)
    from_row = lax.broadcasted_iota(jnp.int32, (t * h, t * h), 1)
    order = (to_row // t == from_row % h) & (to_row % t == from_row // h)
    by_head = dot(jnp.where(order, 1.0, 0.0).astype(jnp.bfloat16), latent)
    for copy in copies[4:]:
        copy.wait()
    for i in range(h):
        out = dot(by_head[i * t : (i + 1) * t].astype(jnp.bfloat16), av_ref[i])
        heads_ref[:, i * vdim : (i + 1) * vdim] = out.astype(jnp.bfloat16)
    res_out_ref[...] = res_ref[...]
    lane = lax.broadcasted_iota(jnp.int32, (t, LANES), 1)
    table = jnp.zeros((t, LANES), jnp.float32)
    for k in range(routes_ref.shape[1]):
        named = lane == routes_ref[:, k : k + 1]
        table = jnp.where(named, weights_ref[:, k : k + 1], table)
    high = table.astype(jnp.bfloat16).astype(jnp.float32)
    low = pltpu.roll(table - high, LANES // 2, 1)
    table_ref[...] = jnp.where(lane < LANES // 2, high, low).astype(jnp.bfloat16)


def pack_kernel(me_ref, heads_ref, res_ref, table_ref, *msgs):
    cols = res_ref.shape[1] // len(msgs)
    width = heads_ref.shape[1]
    me = me_ref[0]
    for step, msg in enumerate(msgs):
        start = pl.multiple_of((me ^ step) * cols, LANES)
        msg[:, :width] = heads_ref[...]
        msg[:, width : width + cols] = res_ref[:, pl.ds(start, cols)]
        msg[:, width + cols :] = table_ref[...]


def stacked(refs, first, last):
    blocks = [ref[:, first:last].astype(jnp.float32) for ref in refs]
    return jnp.concatenate(blocks, axis=0)


def project_kernel(proj_ref, *refs):
    *msgs, out_ref, res_ref, table_ref = refs
    width = proj_ref.shape[0]
    cols = proj_ref.shape[1]
    heads = stacked(msgs, 0, width).astype(jnp.bfloat16)
    out_ref[...] = dot(heads, proj_ref[...]).astype(jnp.bfloat16)
    res_ref[...] = stacked(msgs, width, width + cols)
    table_ref[...] = stacked(msgs, width + cols, width + cols + LANES)


def add_kernel(a_ref, b_ref, out_ref):
    total = a_ref[...].astype(jnp.float32) + b_ref[...].astype(jnp.float32)
    out_ref[...] = total.astype(out_ref.dtype)


def mid_kernel(a_ref, b_ref, res_ref, out_ref):
    total = a_ref[...].astype(jnp.float32) + b_ref[...].astype(jnp.float32)
    attention = total.astype(jnp.bfloat16).astype(jnp.float32)
    out_ref[...] = (res_ref[...] + attention).astype(jnp.bfloat16)


def expert_kernel(experts, me_ref, table_ref, gain_ref, wg_ref, wu_ref, wd_ref, *refs):
    n = (len(refs) - 3) // 2
    mids, (own_ref, total_ref), outs, (mid_ref, sum_ref) = refs[:n], refs[n : n + 2], refs[n + 2 : -2], refs[-2:]
    tokens, cols = mids[0].shape
    rows = tokens // n
    me = me_ref[0]
    squares = jnp.zeros((tokens, 1), jnp.float32)
    for k in range(n):
        got = mids[k][...].astype(jnp.float32)
        block = jnp.concatenate([got[(i ^ k) * rows : (i ^ k) * rows + rows] for i in range(n)], axis=0)
        squares = squares + jnp.sum(block * block, axis=-1, keepdims=True)
        mid_ref[:, pl.ds(pl.multiple_of((me ^ k) * cols, LANES), cols)] = block
    inverse = lax.rsqrt(squares / (n * cols) + 1e-06)
    own_ref[...] = mid_ref[:rows].astype(jnp.bfloat16)
    normed = (mid_ref[...] * inverse * gain_ref[...].reshape(1, n * cols)).astype(jnp.bfloat16)
    lane = lax.broadcasted_iota(jnp.int32, (tokens, LANES), 1) % (LANES // 2)
    for e in range(experts):
        gate = dot(normed, wg_ref[e])
        up = dot(normed, wu_ref[e])
        weight = jnp.sum(
            jnp.where(lane == me * experts + e, table_ref[...], 0.0), axis=1, keepdims=True
        )
        hidden = gate / (1.0 + jnp.exp(-gate)) * up * weight
        hidden = jnp.where(weight != 0.0, hidden, 0.0).astype(jnp.bfloat16)
        down = dot(hidden, wd_ref[e])
        if e == 0:
            sum_ref[...] = down
        else:
            sum_ref[...] += down
    total_ref[...] = sum_ref[:rows]
    for k in range(1, n):
        outs[k - 1][...] = sum_ref[k * rows : (k + 1) * rows].astype(jnp.bfloat16)


def join_kernel(total_ref, *refs):
    *got, out_ref = refs
    total = total_ref[...]
    for ref in got:
        total = total + ref[...].astype(jnp.float32)
    out_ref[...] = total.astype(jnp.bfloat16)


def shards(
    residual,
    query_latent,
    query_rope,
    cache_latent,
    cache_rope,
    absorb_value,
    out_proj,
    norm_gain,
    routes,
    route_weights,
    w_gate,
    w_up,
    w_down,
):
    args = (
        residual,
        query_latent,
        query_rope,
        cache_latent,
        cache_rope,
        absorb_value,
        out_proj,
        norm_gain,
        routes,
        route_weights,
        w_gate,
        w_up,
        w_down,
    )
    n = lax.axis_size("expert")
    head_n = lax.axis_size("head")
    rows, model_d = residual.shape
    width, cols = out_proj.shape
    experts = w_gate.shape[0]
    tokens = rows * n
    fits = rows == ROWS and cols % LANES == 0 and n & (n - 1) == 0 and head_n == 4
    if not fits or experts * n > LANES // 2 or width % LANES:
        return plain_shards(*args)
    scale = (absorb_value.shape[2] + query_rope.shape[2]) ** (-0.5)
    me = lax.axis_index("expert").astype(jnp.int32).reshape(1)

    def in_vmem(x):
        return pltpu.with_memory_space_constraint(x, pltpu.VMEM)

    inputs = [
        query_latent,
        cache_latent,
        query_rope,
        cache_rope,
        absorb_value,
        residual,
        routes,
        route_weights,
    ]
    local = call(
        functools.partial(attend_kernel, scale),
        [bf16(rows, width), bf16(rows, model_d), bf16(rows, LANES)],
        *[pltpu.with_memory_space_constraint(x, pltpu.HBM) for x in inputs],
        limit=6 << 20,
        scratch=[pltpu.VMEM(x.shape, x.dtype) for x in inputs] + [pltpu.SemaphoreType.DMA((len(inputs),))],
        specs=[pl.BlockSpec(memory_space=pltpu.HBM)] * len(inputs),
    )
    msgs = call(
        pack_kernel,
        [bf16(rows, width + cols + LANES)] * n,
        me,
        *local,
        limit=2 << 20,
        specs=[SMEM] + [VMEM] * 3,
        flops=FLOPS[0],
    )
    got = [msgs[0]] + [swap(msgs[k], "expert", n, k) for k in range(1, n)]
    partial, res, table = call(
        project_kernel,
        [bf16(tokens, cols), f32(tokens, cols), f32(tokens, LANES)],
        in_vmem(out_proj),
        *got,
        limit=4 << 20,
        flops=FLOPS[1],
    )
    pair = call(
        add_kernel,
        bf16(tokens, cols),
        partial,
        swap(partial, "head", head_n, 1),
        limit=2 << 20,
        flops=FLOPS[2],
    )
    mid = call(
        mid_kernel,
        bf16(tokens, cols),
        pair,
        swap(pair, "head", head_n, 2),
        res,
        limit=2 << 20,
        flops=FLOPS[3],
    )
    mids = [mid] + [swap(mid, "expert", n, k) for k in range(1, n)]
    own_mid, own, *parts = call(
        functools.partial(expert_kernel, experts),
        [bf16(rows, model_d), f32(rows, model_d)] + [bf16(rows, model_d)] * (n - 1),
        me,
        table,
        norm_gain,
        in_vmem(w_gate),
        in_vmem(w_up),
        in_vmem(w_down),
        *mids,
        limit=8 << 20,
        scratch=[pltpu.VMEM((tokens, model_d), jnp.float32)] * 2,
        specs=[SMEM] + [VMEM] * (5 + n),
        flops=FLOPS[4],
    )
    back = [swap(parts[k - 1], "expert", n, k) for k in range(1, n)]
    mixed = call(join_kernel, bf16(rows, model_d), own, *back, limit=2 << 20)
    for step in (1, 2):
        mixed = call(
            add_kernel,
            bf16(rows, model_d),
            mixed,
            swap(mixed, "head", head_n, step),
            limit=2 << 20,
        )
    return own_mid, mixed


def solution(mesh):
    in_specs = (
        P(("groups", "expert"), None),
        P(("groups", "expert"), "head", None),
        P(("groups", "expert"), "head", None),
        P(("groups", "expert"), None, None),
        P(("groups", "expert"), None, None),
        P("head", None, None),
        P("head", "expert"),
        P(),
        P(("groups", "expert"), None),
        P(("groups", "expert"), None),
        P("expert", None, "head"),
        P("expert", None, "head"),
        P("expert", "head", None),
    )
    out_specs = (P(("groups", "expert"), None), P(("groups", "expert"), None))
    return jax.shard_map(shards, mesh=mesh, in_specs=in_specs, out_specs=out_specs, check_vma=False)
```

```python
import functools

import jax
import jax.numpy as jnp
from jax import lax
from jax.experimental import pallas as pl
from jax.experimental.pallas import tpu as pltpu
from jax.sharding import PartitionSpec as P

LANES = 128
ROWS = 8
VMEM = pl.BlockSpec(memory_space=pltpu.VMEM)
FLOPS = (8 * 10**10, 1, 1, 1, 10**10)


def swap(x, axis, size, step):
    return lax.ppermute(x, axis, [(s, s ^ step) for s in range(size)])


def gather_rows(x, axis):
    size = lax.axis_size(axis)
    me = lax.axis_index(axis)
    out = jnp.zeros((size,) + x.shape, x.dtype)
    out = lax.dynamic_update_index_in_dim(out, x, me, 0)
    for step in range(1, size):
        out = lax.dynamic_update_index_in_dim(out, swap(x, axis, size, step), me ^ step, 0)
    return out


def scatter_sum(blocks, axis):
    size = lax.axis_size(axis)
    me = lax.axis_index(axis)
    total = lax.dynamic_index_in_dim(blocks, me, 0, keepdims=False)
    for step in range(1, size):
        block = lax.dynamic_index_in_dim(blocks, me ^ step, 0, keepdims=False)
        total = total + swap(block.astype(jnp.bfloat16), axis, size, step).astype(jnp.float32)
    return total


def sum_all(x, axis):
    size = lax.axis_size(axis)
    step = 1
    while step < size:
        x = x + swap(x.astype(jnp.bfloat16), axis, size, step).astype(jnp.float32)
        step *= 2
    return x


def attend(query_lat, query_rot, cache_lat, cache_rot, absorb_value, score_scale):
    scores = jnp.einsum("thl,tcl->thc", query_lat, cache_lat, preferred_element_type=jnp.float32)
    scores = scores + jnp.einsum(
        "thr,tcr->thc", query_rot, cache_rot, preferred_element_type=jnp.float32
    )
    probs = jax.nn.softmax(scores * score_scale, axis=-1).astype(jnp.bfloat16)
    latent = jnp.einsum(
        "thc,tcl->thl", probs, cache_lat, preferred_element_type=jnp.float32
    ).astype(jnp.bfloat16)
    per_head = jnp.einsum(
        "thl,hlv->thv", latent, absorb_value, preferred_element_type=jnp.float32
    ).astype(jnp.bfloat16)
    return per_head.reshape(per_head.shape[0], per_head.shape[1] * per_head.shape[2])


def plain_shards(
    residual,
    query_latent,
    query_rope,
    cache_latent,
    cache_rope,
    absorb_value,
    out_proj,
    norm_gain,
    routes,
    route_weights,
    w_gate,
    w_up,
    w_down,
):
    sources = lax.axis_size("expert")
    me = lax.axis_index("expert")
    experts, model_d, hidden_f = w_gate.shape
    rows = residual.shape[0]
    tokens = rows * sources
    score_scale = (absorb_value.shape[2] + query_rope.shape[2]) ** (-0.5)
    all_res = gather_rows(residual, "expert").reshape(tokens, model_d)
    all_routes = gather_rows(routes, "expert").reshape(tokens, -1)
    all_weights = gather_rows(route_weights, "expert").reshape(tokens, -1)
    own_ids = me * experts + jnp.arange(experts, dtype=jnp.int32)
    named = all_routes[:, None, :] == own_ids[None, :, None]
    chosen = jnp.any(named, axis=2)
    weight = jnp.sum(jnp.where(named, all_weights[:, None, :], 0.0), axis=2)

    per_head = attend(
        query_latent, query_rope, cache_latent, cache_rope, absorb_value, score_scale
    )
    all_heads = gather_rows(per_head, "expert").reshape(tokens, -1)
    partial = jnp.dot(all_heads, out_proj, preferred_element_type=jnp.float32)
    summed = sum_all(partial, "head").astype(jnp.bfloat16)
    attention = gather_rows(summed, "expert")
    attention = attention.transpose(1, 0, 2).reshape(tokens, model_d)
    mid = (all_res.astype(jnp.float32) + attention.astype(jnp.float32)).astype(jnp.bfloat16)
    mid_float = mid.astype(jnp.float32)
    normed = (
        mid_float
        * lax.rsqrt(jnp.mean(mid_float * mid_float, axis=-1, keepdims=True) + 1e-06)
        * norm_gain
    ).astype(jnp.bfloat16)
    gate = jnp.einsum("td,edf->etf", normed, w_gate, preferred_element_type=jnp.float32)
    up = jnp.einsum("td,edf->etf", normed, w_up, preferred_element_type=jnp.float32)
    hidden = jnp.where(
        chosen.T[:, :, None], jax.nn.silu(gate) * up * weight.T[:, :, None], 0.0
    ).astype(jnp.bfloat16)
    down = jnp.einsum("etf,efd->td", hidden, w_down, preferred_element_type=jnp.float32)
    mixed = scatter_sum(down.reshape(sources, rows, model_d), "expert")
    mixed = sum_all(mixed, "head").astype(jnp.bfloat16)
    own_mid = lax.dynamic_slice_in_dim(mid, me * rows, rows, 0)
    return own_mid, mixed


def call(body, outs, *args, limit, scratch=(), flops=None, specs=None):
    estimate = None
    if flops is not None:
        estimate = pl.CostEstimate(flops=flops, bytes_accessed=1 << 20, transcendentals=0)
    return pl.pallas_call(
        body,
        out_shape=outs,
        in_specs=[VMEM] * len(args) if specs is None else specs,
        out_specs=jax.tree.map(lambda _: VMEM, outs),
        scratch_shapes=list(scratch),
        compiler_params=pltpu.CompilerParams(vmem_limit_bytes=limit),
        cost_estimate=estimate,
    )(*args)


def bf16(*shape):
    return jax.ShapeDtypeStruct(shape, jnp.bfloat16)


def f32(*shape):
    return jax.ShapeDtypeStruct(shape, jnp.float32)


def dot(a, b):
    return jnp.dot(a, b, preferred_element_type=jnp.float32)


def dot_t(a, b):
    return lax.dot_general(a, b, (((1,), (1,)), ((), ())), preferred_element_type=jnp.float32)


def rows_of(x, first, second):
    return x.astype(jnp.float32).reshape(first * second, x.shape[2]).astype(x.dtype)


def attend_kernel(scale, *refs):
    sources, (heads_ref, res_out_ref, table_ref), held, sems = refs[:8], refs[8:11], refs[11:19], refs[19]
    copies = [
        pltpu.make_async_copy(source, place, sems.at[i])
        for i, (source, place) in enumerate(zip(sources, held))
    ]
    for copy in copies:
        copy.start()
    ql_ref, cl_ref, qr_ref, cr_ref, av_ref, res_ref, routes_ref, weights_ref = held
    t, h, _ = ql_ref.shape
    c = cl_ref.shape[1]
    vdim = av_ref.shape[2]
    for copy in copies[:4]:
        copy.wait()
    cache = rows_of(cl_ref[...], t, c)
    scores = dot_t(rows_of(ql_ref[...], t, h), cache)
    scores = scores + dot_t(rows_of(qr_ref[...], t, h), rows_of(cr_ref[...], t, c))
    row_t = lax.broadcasted_iota(jnp.int32, (t * h, t * c), 0) // h
    col_t = lax.broadcasted_iota(jnp.int32, (t * h, t * c), 1) // c
    scores = jnp.where(row_t == col_t, scores * scale, -jnp.inf)
    top = jnp.max(scores, axis=-1, keepdims=True)
    exps = jnp.exp(scores - top)
    probs = (exps / jnp.sum(exps, axis=-1, keepdims=True)).astype(jnp.bfloat16)
    latent = dot(probs, cache).astype(jnp.bfloat16)
    to_row = lax.broadcasted_iota(jnp.int32, (t * h, t * h), 0)
    from_row = lax.broadcasted_iota(jnp.int32, (t * h, t * h), 1)
    order = (to_row // t == from_row % h) & (to_row % t == from_row // h)
    by_head = dot(jnp.where(order, 1.0, 0.0).astype(jnp.bfloat16), latent)
    for copy in copies[4:]:
        copy.wait()
    for i in range(h):
        out = dot(by_head[i * t : (i + 1) * t].astype(jnp.bfloat16), av_ref[i])
        heads_ref[:, i * vdim : (i + 1) * vdim] = out.astype(jnp.bfloat16)
    res_out_ref[...] = res_ref[...]
    lane = lax.broadcasted_iota(jnp.int32, (t, LANES), 1)
    table = jnp.zeros((t, LANES), jnp.float32)
    for k in range(routes_ref.shape[1]):
        named = lane == routes_ref[:, k : k + 1]
        table = jnp.where(named, weights_ref[:, k : k + 1], table)
    high = table.astype(jnp.bfloat16).astype(jnp.float32)
    low = pltpu.roll(table - high, LANES // 2, 1)
    table_ref[...] = jnp.where(lane < LANES // 2, high, low).astype(jnp.bfloat16)


def pack_kernel(heads_ref, res_ref, table_ref, *msgs):
    cols = res_ref.shape[1] // len(msgs)
    width = heads_ref.shape[1]
    me = lax.axis_index("expert")
    for step, msg in enumerate(msgs):
        start = pl.multiple_of((me ^ step) * cols, LANES)
        msg[:, :width] = heads_ref[...]
        msg[:, width : width + cols] = res_ref[:, pl.ds(start, cols)]
        msg[:, width + cols :] = table_ref[...]


def stacked(refs, first, last):
    blocks = [ref[:, first:last].astype(jnp.float32) for ref in refs]
    return jnp.concatenate(blocks, axis=0)


def project_kernel(proj_ref, *refs):
    *msgs, out_ref, res_ref, table_ref = refs
    msgs = msgs[::-1]
    width = proj_ref.shape[0]
    cols = proj_ref.shape[1]
    heads = stacked(msgs, 0, width).astype(jnp.bfloat16)
    out_ref[...] = dot(heads, proj_ref[...]).astype(jnp.bfloat16)
    res_ref[...] = stacked(msgs, width, width + cols)
    table_ref[...] = stacked(msgs, width + cols, width + cols + LANES)


def add_kernel(a_ref, b_ref, out_ref):
    total = a_ref[...].astype(jnp.float32) + b_ref[...].astype(jnp.float32)
    out_ref[...] = total.astype(out_ref.dtype)


def mid_kernel(a_ref, b_ref, res_ref, out_ref):
    total = a_ref[...].astype(jnp.float32) + b_ref[...].astype(jnp.float32)
    attention = total.astype(jnp.bfloat16).astype(jnp.float32)
    out_ref[...] = (res_ref[...] + attention).astype(jnp.bfloat16)


def expert_kernel(experts, table_ref, gain_ref, wg_ref, wu_ref, wd_ref, *refs):
    n = (len(refs) - 3) // 2
    mids, (own_ref, total_ref), outs, (mid_ref, sum_ref) = refs[:n], refs[n : n + 2], refs[n + 2 : -2], refs[-2:]
    tokens, cols = mids[0].shape
    rows = tokens // n
    me = lax.axis_index("expert")
    squares = jnp.zeros((tokens, 1), jnp.float32)
    for k in range(n):
        got = mids[k][...].astype(jnp.float32)
        block = jnp.concatenate([got[(i ^ k) * rows : (i ^ k) * rows + rows] for i in range(n)], axis=0)
        squares = squares + jnp.sum(block * block, axis=-1, keepdims=True)
        mid_ref[:, pl.ds(pl.multiple_of((me ^ k) * cols, LANES), cols)] = block
    inverse = lax.rsqrt(squares / (n * cols) + 1e-06)
    own_ref[...] = mid_ref[:rows].astype(jnp.bfloat16)
    normed = (mid_ref[...] * inverse * gain_ref[...].reshape(1, n * cols)).astype(jnp.bfloat16)
    copies = max(1, LANES // tokens)
    normed = jnp.concatenate([normed] * copies, axis=0)
    lane = lax.broadcasted_iota(jnp.int32, (tokens, LANES), 1) % (LANES // 2)
    for e in range(experts):
        gate = dot(normed, wg_ref[e])[:tokens]
        up = dot(normed, wu_ref[e])[:tokens]
        weight = jnp.sum(
            jnp.where(lane == me * experts + e, table_ref[...], 0.0), axis=1, keepdims=True
        )
        hidden = gate / (1.0 + jnp.exp(-gate)) * up * weight
        hidden = jnp.where(weight != 0.0, hidden, 0.0).astype(jnp.bfloat16)
        hidden = jnp.concatenate([hidden] * copies, axis=0)
        down = dot(hidden, wd_ref[e])[:tokens]
        if e == 0:
            sum_ref[...] = down
        else:
            sum_ref[...] += down
    total_ref[...] = sum_ref[:rows]
    for k in range(1, n):
        outs[k - 1][...] = sum_ref[k * rows : (k + 1) * rows].astype(jnp.bfloat16)


def join_kernel(total_ref, *refs):
    *got, out_ref = refs
    total = total_ref[...]
    for ref in got:
        total = total + ref[...].astype(jnp.float32)
    out_ref[...] = total.astype(jnp.bfloat16)


def shards(
    residual,
    query_latent,
    query_rope,
    cache_latent,
    cache_rope,
    absorb_value,
    out_proj,
    norm_gain,
    routes,
    route_weights,
    w_gate,
    w_up,
    w_down,
):
    args = (
        residual,
        query_latent,
        query_rope,
        cache_latent,
        cache_rope,
        absorb_value,
        out_proj,
        norm_gain,
        routes,
        route_weights,
        w_gate,
        w_up,
        w_down,
    )
    n = lax.axis_size("expert")
    head_n = lax.axis_size("head")
    rows, model_d = residual.shape
    width, cols = out_proj.shape
    experts = w_gate.shape[0]
    tokens = rows * n
    fits = rows == ROWS and cols % LANES == 0 and n & (n - 1) == 0 and head_n == 4
    if not fits or experts * n > LANES // 2 or width % LANES:
        return plain_shards(*args)
    scale = (absorb_value.shape[2] + query_rope.shape[2]) ** (-0.5)
    def in_vmem(x):
        return pltpu.with_memory_space_constraint(x, pltpu.VMEM)

    inputs = [
        query_latent,
        cache_latent,
        query_rope,
        cache_rope,
        absorb_value,
        residual,
        routes,
        route_weights,
    ]
    local = call(
        functools.partial(attend_kernel, scale),
        [bf16(rows, width), bf16(rows, model_d), bf16(rows, LANES)],
        *[pltpu.with_memory_space_constraint(x, pltpu.HBM) for x in inputs],
        limit=6 << 20,
        scratch=[pltpu.VMEM(x.shape, x.dtype) for x in inputs] + [pltpu.SemaphoreType.DMA((len(inputs),))],
        specs=[pl.BlockSpec(memory_space=pltpu.HBM)] * len(inputs),
    )
    msgs = call(
        pack_kernel,
        [bf16(rows, width + cols + LANES)] * n,
        *local,
        limit=2 << 20,
        flops=FLOPS[0],
    )
    got = [swap(msgs[k], "expert", n, k) for k in range(n - 1, 0, -1)] + [msgs[0]]
    partial, res, table = call(
        project_kernel,
        [bf16(tokens, cols), f32(tokens, cols), f32(tokens, LANES)],
        in_vmem(out_proj),
        *got,
        limit=4 << 20,
        flops=FLOPS[1],
    )
    pair = call(
        add_kernel,
        bf16(tokens, cols),
        partial,
        swap(partial, "head", head_n, 1),
        limit=2 << 20,
        flops=FLOPS[2],
    )
    mid = call(
        mid_kernel,
        bf16(tokens, cols),
        pair,
        swap(pair, "head", head_n, 2),
        res,
        limit=2 << 20,
        flops=FLOPS[3],
    )
    mids = [mid] + [swap(mid, "expert", n, k) for k in range(1, n)]
    own_mid, own, *parts = call(
        functools.partial(expert_kernel, experts),
        [bf16(rows, model_d), f32(rows, model_d)] + [bf16(rows, model_d)] * (n - 1),
        table,
        norm_gain,
        in_vmem(w_gate),
        in_vmem(w_up),
        in_vmem(w_down),
        *mids,
        limit=8 << 20,
        scratch=[pltpu.VMEM((tokens, model_d), jnp.float32)] * 2,
        flops=FLOPS[4],
    )
    back = [swap(parts[k - 1], "expert", n, k) for k in range(n - 1, 0, -1)]
    mixed = call(join_kernel, bf16(rows, model_d), own, *back, limit=2 << 20)
    for step in (1, 2):
        mixed = call(
            add_kernel,
            bf16(rows, model_d),
            mixed,
            swap(mixed, "head", head_n, step),
            limit=2 << 20,
        )
    return own_mid, mixed


def solution(mesh):
    in_specs = (
        P(("groups", "expert"), None),
        P(("groups", "expert"), "head", None),
        P(("groups", "expert"), "head", None),
        P(("groups", "expert"), None, None),
        P(("groups", "expert"), None, None),
        P("head", None, None),
        P("head", "expert"),
        P(),
        P(("groups", "expert"), None),
        P(("groups", "expert"), None),
        P("expert", None, "head"),
        P("expert", None, "head"),
        P("expert", "head", None),
    )
    out_specs = (P(("groups", "expert"), None), P(("groups", "expert"), None))
    return jax.shard_map(shards, mesh=mesh, in_specs=in_specs, out_specs=out_specs, check_vma=False)
```

```python
import functools

import jax
import jax.numpy as jnp
from jax import lax
from jax.experimental import pallas as pl
from jax.experimental.pallas import tpu as pltpu
from jax.sharding import PartitionSpec as P

LANES = 128
LIMIT = 4 << 20
AHEAD = 3
ROWS = 8
VMEM = pl.BlockSpec(memory_space=pltpu.VMEM)
FLOPS = (16 * 10**10, 1, 1, 1, 10**9, 10**9)


def swap(x, axis, size, step):
    return lax.ppermute(x, axis, [(s, s ^ step) for s in range(size)])


def gather_rows(x, axis):
    size = lax.axis_size(axis)
    me = lax.axis_index(axis)
    out = jnp.zeros((size,) + x.shape, x.dtype)
    out = lax.dynamic_update_index_in_dim(out, x, me, 0)
    for step in range(1, size):
        out = lax.dynamic_update_index_in_dim(out, swap(x, axis, size, step), me ^ step, 0)
    return out


def scatter_sum(blocks, axis):
    size = lax.axis_size(axis)
    me = lax.axis_index(axis)
    total = lax.dynamic_index_in_dim(blocks, me, 0, keepdims=False)
    for step in range(1, size):
        block = lax.dynamic_index_in_dim(blocks, me ^ step, 0, keepdims=False)
        total = total + swap(block.astype(jnp.bfloat16), axis, size, step).astype(jnp.float32)
    return total


def sum_all(x, axis):
    size = lax.axis_size(axis)
    step = 1
    while step < size:
        x = x + swap(x.astype(jnp.bfloat16), axis, size, step).astype(jnp.float32)
        step *= 2
    return x


def attend(query_lat, query_rot, cache_lat, cache_rot, absorb_value, score_scale):
    scores = jnp.einsum("thl,tcl->thc", query_lat, cache_lat, preferred_element_type=jnp.float32)
    scores = scores + jnp.einsum(
        "thr,tcr->thc", query_rot, cache_rot, preferred_element_type=jnp.float32
    )
    probs = jax.nn.softmax(scores * score_scale, axis=-1).astype(jnp.bfloat16)
    latent = jnp.einsum(
        "thc,tcl->thl", probs, cache_lat, preferred_element_type=jnp.float32
    ).astype(jnp.bfloat16)
    per_head = jnp.einsum(
        "thl,hlv->thv", latent, absorb_value, preferred_element_type=jnp.float32
    ).astype(jnp.bfloat16)
    return per_head.reshape(per_head.shape[0], per_head.shape[1] * per_head.shape[2])


def plain_shards(
    residual,
    query_latent,
    query_rope,
    cache_latent,
    cache_rope,
    absorb_value,
    out_proj,
    norm_gain,
    routes,
    route_weights,
    w_gate,
    w_up,
    w_down,
):
    sources = lax.axis_size("expert")
    me = lax.axis_index("expert")
    experts, model_d, hidden_f = w_gate.shape
    rows = residual.shape[0]
    tokens = rows * sources
    score_scale = (absorb_value.shape[2] + query_rope.shape[2]) ** (-0.5)
    all_res = gather_rows(residual, "expert").reshape(tokens, model_d)
    all_routes = gather_rows(routes, "expert").reshape(tokens, -1)
    all_weights = gather_rows(route_weights, "expert").reshape(tokens, -1)
    own_ids = me * experts + jnp.arange(experts, dtype=jnp.int32)
    named = all_routes[:, None, :] == own_ids[None, :, None]
    chosen = jnp.any(named, axis=2)
    weight = jnp.sum(jnp.where(named, all_weights[:, None, :], 0.0), axis=2)

    per_head = attend(
        query_latent, query_rope, cache_latent, cache_rope, absorb_value, score_scale
    )
    all_heads = gather_rows(per_head, "expert").reshape(tokens, -1)
    partial = jnp.dot(all_heads, out_proj, preferred_element_type=jnp.float32)
    summed = sum_all(partial, "head").astype(jnp.bfloat16)
    attention = gather_rows(summed, "expert")
    attention = attention.transpose(1, 0, 2).reshape(tokens, model_d)
    mid = (all_res.astype(jnp.float32) + attention.astype(jnp.float32)).astype(jnp.bfloat16)
    mid_float = mid.astype(jnp.float32)
    normed = (
        mid_float
        * lax.rsqrt(jnp.mean(mid_float * mid_float, axis=-1, keepdims=True) + 1e-06)
        * norm_gain
    ).astype(jnp.bfloat16)
    gate = jnp.einsum("td,edf->etf", normed, w_gate, preferred_element_type=jnp.float32)
    up = jnp.einsum("td,edf->etf", normed, w_up, preferred_element_type=jnp.float32)
    hidden = jnp.where(
        chosen.T[:, :, None], jax.nn.silu(gate) * up * weight.T[:, :, None], 0.0
    ).astype(jnp.bfloat16)
    down = jnp.einsum("etf,efd->td", hidden, w_down, preferred_element_type=jnp.float32)
    mixed = scatter_sum(down.reshape(sources, rows, model_d), "expert")
    mixed = sum_all(mixed, "head").astype(jnp.bfloat16)
    own_mid = lax.dynamic_slice_in_dim(mid, me * rows, rows, 0)
    return own_mid, mixed


def call(body, outs, *args, limit, scratch=(), flops=None, specs=None):
    estimate = None
    if flops is not None:
        estimate = pl.CostEstimate(flops=flops, bytes_accessed=1 << 20, transcendentals=0)
    return pl.pallas_call(
        body,
        out_shape=outs,
        in_specs=[VMEM] * len(args) if specs is None else specs,
        out_specs=jax.tree.map(lambda _: VMEM, outs),
        scratch_shapes=list(scratch),
        compiler_params=pltpu.CompilerParams(vmem_limit_bytes=limit),
        cost_estimate=estimate,
    )(*args)


def bf16(*shape):
    return jax.ShapeDtypeStruct(shape, jnp.bfloat16)


def f32(*shape):
    return jax.ShapeDtypeStruct(shape, jnp.float32)


def dot(a, b):
    return jnp.dot(a, b, preferred_element_type=jnp.float32)


def dot_t(a, b):
    return lax.dot_general(a, b, (((1,), (1,)), ((), ())), preferred_element_type=jnp.float32)


def rows_of(x, first, second):
    return x.astype(jnp.float32).reshape(first * second, x.shape[2]).astype(x.dtype)


def attend_kernel(scale, *refs):
    sources, outs, held, sems = refs[:9], refs[9:13], refs[13:22], refs[22]
    heads_ref, res_out_ref, table_ref, gain_out_ref = outs
    copies = [
        pltpu.make_async_copy(source, place, sems.at[i])
        for i, (source, place) in enumerate(zip(sources, held))
    ]
    for copy in copies:
        copy.start()
    ql_ref, cl_ref, qr_ref, cr_ref, av_ref, res_ref, routes_ref, weights_ref, gain_ref = held
    t, h, _ = ql_ref.shape
    c = cl_ref.shape[1]
    vdim = av_ref.shape[2]
    for copy in copies[:4]:
        copy.wait()
    cache = rows_of(cl_ref[...], t, c)
    scores = dot_t(rows_of(ql_ref[...], t, h), cache)
    scores = scores + dot_t(rows_of(qr_ref[...], t, h), rows_of(cr_ref[...], t, c))
    row_t = lax.broadcasted_iota(jnp.int32, (t * h, t * c), 0) // h
    col_t = lax.broadcasted_iota(jnp.int32, (t * h, t * c), 1) // c
    scores = jnp.where(row_t == col_t, scores * scale, -jnp.inf)
    top = jnp.max(scores, axis=-1, keepdims=True)
    exps = jnp.exp(scores - top)
    probs = (exps / jnp.sum(exps, axis=-1, keepdims=True)).astype(jnp.bfloat16)
    latent = dot(probs, cache).astype(jnp.bfloat16)
    to_row = lax.broadcasted_iota(jnp.int32, (t * h, t * h), 0)
    from_row = lax.broadcasted_iota(jnp.int32, (t * h, t * h), 1)
    order = (to_row // t == from_row % h) & (to_row % t == from_row // h)
    by_head = dot(jnp.where(order, 1.0, 0.0).astype(jnp.bfloat16), latent)
    for copy in copies[4:]:
        copy.wait()
    for i in range(h):
        out = dot(by_head[i * t : (i + 1) * t].astype(jnp.bfloat16), av_ref[i])
        heads_ref[:, i * vdim : (i + 1) * vdim] = out.astype(jnp.bfloat16)
    res_out_ref[...] = res_ref[...]
    gain_out_ref[...] = gain_ref[...].reshape(gain_out_ref.shape)
    lane = lax.broadcasted_iota(jnp.int32, (t, LANES), 1)
    table = jnp.zeros((t, LANES), jnp.float32)
    for k in range(routes_ref.shape[1]):
        named = lane == routes_ref[:, k : k + 1]
        table = jnp.where(named, weights_ref[:, k : k + 1], table)
    high = table.astype(jnp.bfloat16).astype(jnp.float32)
    low = pltpu.roll(table - high, LANES // 2, 1)
    table_ref[...] = jnp.where(lane < LANES // 2, high, low).astype(jnp.bfloat16)


def pack_kernel(heads_ref, res_ref, table_ref, *msgs):
    cols = res_ref.shape[1] // len(msgs)
    width = heads_ref.shape[1]
    me = lax.axis_index("expert")
    for step, msg in enumerate(msgs):
        start = pl.multiple_of((me ^ step) * cols, LANES)
        msg[:, :width] = heads_ref[...]
        msg[:, width : width + cols] = res_ref[:, pl.ds(start, cols)]
        msg[:, width + cols :] = table_ref[...]


def stacked(refs, first, last):
    blocks = [ref[:, first:last].astype(jnp.float32) for ref in refs]
    return jnp.concatenate(blocks, axis=0)


def project_kernel(proj_ref, *refs):
    *msgs, out_ref, res_ref, table_ref = refs
    msgs = msgs[::-1]
    width = proj_ref.shape[0]
    cols = proj_ref.shape[1]
    heads = stacked(msgs, 0, width).astype(jnp.bfloat16)
    out_ref[...] = dot(heads, proj_ref[...]).astype(jnp.bfloat16)
    res_ref[...] = stacked(msgs, width, width + cols)
    table_ref[...] = stacked(msgs, width + cols, width + cols + LANES)


def add_kernel(a_ref, b_ref, out_ref):
    total = a_ref[...].astype(jnp.float32) + b_ref[...].astype(jnp.float32)
    out_ref[...] = total.astype(out_ref.dtype)


def mid_kernel(a_ref, b_ref, res_ref, out_ref):
    total = a_ref[...].astype(jnp.float32) + b_ref[...].astype(jnp.float32)
    attention = total.astype(jnp.bfloat16).astype(jnp.float32)
    out_ref[...] = (res_ref[...] + attention).astype(jnp.bfloat16)


def padded(x):
    return jnp.concatenate([x] * max(1, LANES // x.shape[0]), axis=0)


def add_block(n, k, mid_ref, gain_ref, wg_ref, wu_ref, before, after):
    gate_ref, up_ref, square_ref = after
    tokens, cols = mid_ref.shape
    experts, _, width = wg_ref.shape
    rows = tokens // n
    start = pl.multiple_of((lax.axis_index("expert") ^ k) * cols, LANES)
    got = mid_ref[...].astype(jnp.float32)
    block = jnp.concatenate([got[(i ^ k) * rows : (i ^ k) * rows + rows] for i in range(n)], axis=0)
    square = jnp.sum(block * block, axis=-1, keepdims=True)
    square_ref[...] = square + before[2][...] if before else jnp.broadcast_to(square, square_ref.shape)
    left = padded((block * gain_ref[:, pl.ds(start, cols)]).astype(jnp.bfloat16))
    for e in range(experts):
        at = slice(e * width, (e + 1) * width)
        gate = dot(left, wg_ref[e, pl.ds(start, cols)])[:tokens]
        up = dot(left, wu_ref[e, pl.ds(start, cols)])[:tokens]
        gate_ref[:, at] = gate + before[0][:, at] if before else gate
        up_ref[:, at] = up + before[1][:, at] if before else up


def part_kernel(n, k, gain_ref, wg_ref, wu_ref, _, mid_ref, *refs):
    add_block(n, k, mid_ref, gain_ref, wg_ref, wu_ref, refs[:-3], refs[-3:])


def rest_kernel(n, rest, gain_ref, wg_ref, wu_ref, wd_ref, table_ref, *refs):
    mids, sums, refs = refs[:n], refs[n : n + 3], refs[n + 3 :]
    (own_ref, total_ref), outs = refs[:2], refs[2 : n + 1]
    gate_ref, up_ref, square_ref, sum_ref = refs[n + 1 :]
    tokens, cols = mids[0].shape
    experts, width, _ = wd_ref.shape
    rows = tokens // n
    me = lax.axis_index("expert")
    for k in rest:
        add_block(n, k, mids[k], gain_ref, wg_ref, wu_ref, sums, (gate_ref, up_ref, square_ref))
        sums = (gate_ref, up_ref, square_ref)
    for k in range(n):
        got = mids[k][...].astype(jnp.float32)[k * rows : (k + 1) * rows]
        own_ref[:, pl.ds(pl.multiple_of((me ^ k) * cols, LANES), cols)] = got.astype(jnp.bfloat16)
    inverse = lax.rsqrt(square_ref[:, :1] / (n * cols) + 1e-06)
    lane = lax.broadcasted_iota(jnp.int32, (tokens, LANES), 1) % (LANES // 2)
    for e in range(experts):
        at = slice(e * width, (e + 1) * width)
        gate = gate_ref[:, at] * inverse
        up = up_ref[:, at] * inverse
        weight = jnp.sum(
            jnp.where(lane == me * experts + e, table_ref[...], 0.0), axis=1, keepdims=True
        )
        hidden = gate / (1.0 + jnp.exp(-gate)) * up * weight
        hidden = jnp.where(weight != 0.0, hidden, 0.0).astype(jnp.bfloat16)
        down = dot(padded(hidden), wd_ref[e])[:tokens]
        if e == 0:
            sum_ref[...] = down
        else:
            sum_ref[...] += down
    total_ref[...] = sum_ref[:rows]
    for k in range(1, n):
        outs[k - 1][...] = sum_ref[k * rows : (k + 1) * rows].astype(jnp.bfloat16)


def join_kernel(total_ref, *refs):
    *got, out_ref = refs
    total = total_ref[...]
    for ref in got:
        total = total + ref[...].astype(jnp.float32)
    out_ref[...] = total.astype(jnp.bfloat16)


def shards(
    residual,
    query_latent,
    query_rope,
    cache_latent,
    cache_rope,
    absorb_value,
    out_proj,
    norm_gain,
    routes,
    route_weights,
    w_gate,
    w_up,
    w_down,
):
    args = (
        residual,
        query_latent,
        query_rope,
        cache_latent,
        cache_rope,
        absorb_value,
        out_proj,
        norm_gain,
        routes,
        route_weights,
        w_gate,
        w_up,
        w_down,
    )
    n = lax.axis_size("expert")
    head_n = lax.axis_size("head")
    rows, model_d = residual.shape
    width, cols = out_proj.shape
    experts, _, hidden_f = w_gate.shape
    tokens = rows * n
    fits = rows == ROWS and cols % LANES == 0 and n & (n - 1) == 0 and head_n == 4
    if not fits or experts * n > LANES // 2 or width % LANES:
        return plain_shards(*args)
    scale = (absorb_value.shape[2] + query_rope.shape[2]) ** (-0.5)
    def in_vmem(x):
        return pltpu.with_memory_space_constraint(x, pltpu.VMEM)

    inputs = [
        query_latent,
        cache_latent,
        query_rope,
        cache_rope,
        absorb_value,
        residual,
        routes,
        route_weights,
        norm_gain,
    ]
    *local, gain = call(
        functools.partial(attend_kernel, scale),
        [bf16(rows, width), bf16(rows, model_d), bf16(rows, LANES), f32(1, model_d)],
        *[pltpu.with_memory_space_constraint(x, pltpu.HBM) for x in inputs],
        limit=6 << 20,
        scratch=[pltpu.VMEM(x.shape, x.dtype) for x in inputs] + [pltpu.SemaphoreType.DMA((len(inputs),))],
        specs=[pl.BlockSpec(memory_space=pltpu.HBM)] * len(inputs),
    )
    msgs = call(
        pack_kernel,
        [bf16(rows, width + cols + LANES)] * n,
        *local,
        limit=LIMIT,
        flops=FLOPS[0],
    )
    got = [swap(msgs[k], "expert", n, k) for k in range(n - 1, 0, -1)] + [msgs[0]]
    partial, res, table = call(
        project_kernel,
        [bf16(tokens, cols), f32(tokens, cols), f32(tokens, LANES)],
        in_vmem(out_proj),
        *got,
        limit=LIMIT,
        flops=FLOPS[1],
    )
    pair = call(
        add_kernel,
        bf16(tokens, cols),
        partial,
        swap(partial, "head", head_n, 1),
        limit=LIMIT,
        flops=FLOPS[2],
    )
    mid = call(
        mid_kernel,
        bf16(tokens, cols),
        pair,
        swap(pair, "head", head_n, 2),
        res,
        limit=LIMIT,
        flops=FLOPS[3],
    )
    mids = [mid] + [swap(mid, "expert", n, k) for k in range(1, n)]
    gate_weights, up_weights, down_weights = in_vmem(w_gate), in_vmem(w_up), in_vmem(w_down)
    sum_shapes = [f32(tokens, experts * hidden_f)] * 2 + [f32(tokens, LANES)]
    order = [0] + list(range(n - 1, 0, -1))
    sums = []
    for k in order[:AHEAD]:
        sums = call(
            functools.partial(part_kernel, n, k),
            sum_shapes,
            gain,
            gate_weights,
            up_weights,
            down_weights,
            mids[k],
            *sums,
            limit=LIMIT,
            flops=FLOPS[4],
        )
    own_mid, own, *parts = call(
        functools.partial(rest_kernel, n, order[AHEAD:]),
        [bf16(rows, model_d), f32(rows, model_d)] + [bf16(rows, model_d)] * (n - 1),
        gain,
        gate_weights,
        up_weights,
        down_weights,
        table,
        *mids,
        *sums,
        limit=LIMIT,
        scratch=[pltpu.VMEM(x.shape, x.dtype) for x in sum_shapes + [f32(tokens, model_d)]],
        flops=FLOPS[5],
    )
    back = [swap(parts[k - 1], "expert", n, k) for k in range(n - 1, 0, -1)]
    mixed = call(join_kernel, bf16(rows, model_d), own, *back, limit=LIMIT)
    for step in (1, 2):
        mixed = call(
            add_kernel,
            bf16(rows, model_d),
            mixed,
            swap(mixed, "head", head_n, step),
            limit=LIMIT,
        )
    return own_mid, mixed


def solution(mesh):
    in_specs = (
        P(("groups", "expert"), None),
        P(("groups", "expert"), "head", None),
        P(("groups", "expert"), "head", None),
        P(("groups", "expert"), None, None),
        P(("groups", "expert"), None, None),
        P("head", None, None),
        P("head", "expert"),
        P(),
        P(("groups", "expert"), None),
        P(("groups", "expert"), None),
        P("expert", None, "head"),
        P("expert", None, "head"),
        P("expert", "head", None),
    )
    out_specs = (P(("groups", "expert"), None), P(("groups", "expert"), None))
    return jax.shard_map(shards, mesh=mesh, in_specs=in_specs, out_specs=out_specs, check_vma=False)
```

```python
import functools

import jax
import jax.numpy as jnp
from jax import lax
from jax.experimental import pallas as pl
from jax.experimental.pallas import tpu as pltpu
from jax.sharding import PartitionSpec as P

LANES = 128
LIMIT = 4 << 20
AHEAD = 3
ROWS = 8
VMEM = pl.BlockSpec(memory_space=pltpu.VMEM)
FLOPS = (16 * 10**10, 1, 1, 1, 10**9, 10**9)


def swap(x, axis, size, step):
    return lax.ppermute(x, axis, [(s, s ^ step) for s in range(size)])


def gather_rows(x, axis):
    size = lax.axis_size(axis)
    me = lax.axis_index(axis)
    out = jnp.zeros((size,) + x.shape, x.dtype)
    out = lax.dynamic_update_index_in_dim(out, x, me, 0)
    for step in range(1, size):
        out = lax.dynamic_update_index_in_dim(out, swap(x, axis, size, step), me ^ step, 0)
    return out


def scatter_sum(blocks, axis):
    size = lax.axis_size(axis)
    me = lax.axis_index(axis)
    total = lax.dynamic_index_in_dim(blocks, me, 0, keepdims=False)
    for step in range(1, size):
        block = lax.dynamic_index_in_dim(blocks, me ^ step, 0, keepdims=False)
        total = total + swap(block.astype(jnp.bfloat16), axis, size, step).astype(jnp.float32)
    return total


def sum_all(x, axis):
    size = lax.axis_size(axis)
    step = 1
    while step < size:
        x = x + swap(x.astype(jnp.bfloat16), axis, size, step).astype(jnp.float32)
        step *= 2
    return x


def attend(query_lat, query_rot, cache_lat, cache_rot, absorb_value, score_scale):
    scores = jnp.einsum("thl,tcl->thc", query_lat, cache_lat, preferred_element_type=jnp.float32)
    scores = scores + jnp.einsum(
        "thr,tcr->thc", query_rot, cache_rot, preferred_element_type=jnp.float32
    )
    probs = jax.nn.softmax(scores * score_scale, axis=-1).astype(jnp.bfloat16)
    latent = jnp.einsum(
        "thc,tcl->thl", probs, cache_lat, preferred_element_type=jnp.float32
    ).astype(jnp.bfloat16)
    per_head = jnp.einsum(
        "thl,hlv->thv", latent, absorb_value, preferred_element_type=jnp.float32
    ).astype(jnp.bfloat16)
    return per_head.reshape(per_head.shape[0], per_head.shape[1] * per_head.shape[2])


def plain_shards(
    residual,
    query_latent,
    query_rope,
    cache_latent,
    cache_rope,
    absorb_value,
    out_proj,
    norm_gain,
    routes,
    route_weights,
    w_gate,
    w_up,
    w_down,
):
    sources = lax.axis_size("expert")
    me = lax.axis_index("expert")
    experts, model_d, hidden_f = w_gate.shape
    rows = residual.shape[0]
    tokens = rows * sources
    score_scale = (absorb_value.shape[2] + query_rope.shape[2]) ** (-0.5)
    all_res = gather_rows(residual, "expert").reshape(tokens, model_d)
    all_routes = gather_rows(routes, "expert").reshape(tokens, -1)
    all_weights = gather_rows(route_weights, "expert").reshape(tokens, -1)
    own_ids = me * experts + jnp.arange(experts, dtype=jnp.int32)
    named = all_routes[:, None, :] == own_ids[None, :, None]
    chosen = jnp.any(named, axis=2)
    weight = jnp.sum(jnp.where(named, all_weights[:, None, :], 0.0), axis=2)

    per_head = attend(
        query_latent, query_rope, cache_latent, cache_rope, absorb_value, score_scale
    )
    all_heads = gather_rows(per_head, "expert").reshape(tokens, -1)
    partial = jnp.dot(all_heads, out_proj, preferred_element_type=jnp.float32)
    summed = sum_all(partial, "head").astype(jnp.bfloat16)
    attention = gather_rows(summed, "expert")
    attention = attention.transpose(1, 0, 2).reshape(tokens, model_d)
    mid = (all_res.astype(jnp.float32) + attention.astype(jnp.float32)).astype(jnp.bfloat16)
    mid_float = mid.astype(jnp.float32)
    normed = (
        mid_float
        * lax.rsqrt(jnp.mean(mid_float * mid_float, axis=-1, keepdims=True) + 1e-06)
        * norm_gain
    ).astype(jnp.bfloat16)
    gate = jnp.einsum("td,edf->etf", normed, w_gate, preferred_element_type=jnp.float32)
    up = jnp.einsum("td,edf->etf", normed, w_up, preferred_element_type=jnp.float32)
    hidden = jnp.where(
        chosen.T[:, :, None], jax.nn.silu(gate) * up * weight.T[:, :, None], 0.0
    ).astype(jnp.bfloat16)
    down = jnp.einsum("etf,efd->td", hidden, w_down, preferred_element_type=jnp.float32)
    mixed = scatter_sum(down.reshape(sources, rows, model_d), "expert")
    mixed = sum_all(mixed, "head").astype(jnp.bfloat16)
    own_mid = lax.dynamic_slice_in_dim(mid, me * rows, rows, 0)
    return own_mid, mixed


def call(body, outs, *args, limit, scratch=(), flops=None, specs=None):
    estimate = None
    if flops is not None:
        estimate = pl.CostEstimate(flops=flops, bytes_accessed=1 << 20, transcendentals=0)
    return pl.pallas_call(
        body,
        out_shape=outs,
        in_specs=[VMEM] * len(args) if specs is None else specs,
        out_specs=jax.tree.map(lambda _: VMEM, outs),
        scratch_shapes=list(scratch),
        compiler_params=pltpu.CompilerParams(vmem_limit_bytes=limit),
        cost_estimate=estimate,
    )(*args)


def bf16(*shape):
    return jax.ShapeDtypeStruct(shape, jnp.bfloat16)


def f32(*shape):
    return jax.ShapeDtypeStruct(shape, jnp.float32)


def dot(a, b):
    return jnp.dot(a, b, preferred_element_type=jnp.float32)


def dot_t(a, b):
    return lax.dot_general(a, b, (((1,), (1,)), ((), ())), preferred_element_type=jnp.float32)


def rows_of(x, first, second):
    return x.astype(jnp.float32).reshape(first * second, x.shape[2]).astype(x.dtype)


def attend_kernel(scale, *refs):
    sources, outs, held, sems = refs[:9], refs[9:13], refs[13:22], refs[22]
    heads_ref, res_out_ref, table_ref, gain_out_ref = outs
    copies = [
        pltpu.make_async_copy(source, place, sems.at[i])
        for i, (source, place) in enumerate(zip(sources, held))
    ]
    for copy in copies:
        copy.start()
    ql_ref, cl_ref, qr_ref, cr_ref, av_ref, res_ref, routes_ref, weights_ref, gain_ref = held
    t, h, _ = ql_ref.shape
    c = cl_ref.shape[1]
    vdim = av_ref.shape[2]
    for copy in copies[:4]:
        copy.wait()
    cache = rows_of(cl_ref[...], t, c)
    scores = dot_t(rows_of(ql_ref[...], t, h), cache)
    scores = scores + dot_t(rows_of(qr_ref[...], t, h), rows_of(cr_ref[...], t, c))
    row_t = lax.broadcasted_iota(jnp.int32, (t * h, t * c), 0) // h
    col_t = lax.broadcasted_iota(jnp.int32, (t * h, t * c), 1) // c
    scores = jnp.where(row_t == col_t, scores * scale, -jnp.inf)
    top = jnp.max(scores, axis=-1, keepdims=True)
    exps = jnp.exp(scores - top)
    probs = (exps / jnp.sum(exps, axis=-1, keepdims=True)).astype(jnp.bfloat16)
    latent = dot(probs, cache).astype(jnp.bfloat16)
    to_row = lax.broadcasted_iota(jnp.int32, (t * h, t * h), 0)
    from_row = lax.broadcasted_iota(jnp.int32, (t * h, t * h), 1)
    order = (to_row // t == from_row % h) & (to_row % t == from_row // h)
    by_head = dot(jnp.where(order, 1.0, 0.0).astype(jnp.bfloat16), latent)
    for copy in copies[4:]:
        copy.wait()
    for i in range(h):
        out = dot(by_head[i * t : (i + 1) * t].astype(jnp.bfloat16), av_ref[i])
        heads_ref[:, i * vdim : (i + 1) * vdim] = out.astype(jnp.bfloat16)
    res_out_ref[...] = res_ref[...]
    gain_out_ref[...] = gain_ref[...].reshape(gain_out_ref.shape)
    lane = lax.broadcasted_iota(jnp.int32, (t, LANES), 1)
    table = jnp.zeros((t, LANES), jnp.float32)
    for k in range(routes_ref.shape[1]):
        named = lane == routes_ref[:, k : k + 1]
        table = jnp.where(named, weights_ref[:, k : k + 1], table)
    high = table.astype(jnp.bfloat16).astype(jnp.float32)
    low = pltpu.roll(table - high, LANES // 2, 1)
    table_ref[...] = jnp.where(lane < LANES // 2, high, low).astype(jnp.bfloat16)


def pack_kernel(heads_ref, res_ref, table_ref, *msgs):
    cols = res_ref.shape[1] // len(msgs)
    width = heads_ref.shape[1]
    me = lax.axis_index("expert")
    for step, msg in enumerate(msgs):
        start = pl.multiple_of((me ^ step) * cols, LANES)
        msg[:, :width] = heads_ref[...]
        msg[:, width : width + cols] = res_ref[:, pl.ds(start, cols)]
        msg[:, width + cols :] = table_ref[...]


def stacked(refs, first, last):
    blocks = [ref[:, first:last].astype(jnp.float32) for ref in refs]
    return jnp.concatenate(blocks, axis=0)


def project_kernel(proj_ref, *refs):
    *msgs, out_ref, res_ref, table_ref = refs
    msgs = msgs[::-1]
    width = proj_ref.shape[0]
    cols = proj_ref.shape[1]
    heads = stacked(msgs, 0, width).astype(jnp.bfloat16)
    out_ref[...] = dot(heads, proj_ref[...]).astype(jnp.bfloat16)
    res_ref[...] = stacked(msgs, width, width + cols)
    table_ref[...] = stacked(msgs, width + cols, width + cols + LANES)


def add_kernel(a_ref, b_ref, out_ref):
    total = a_ref[...].astype(jnp.float32) + b_ref[...].astype(jnp.float32)
    out_ref[...] = total.astype(out_ref.dtype)


def mid_kernel(a_ref, b_ref, res_ref, out_ref):
    total = a_ref[...].astype(jnp.float32) + b_ref[...].astype(jnp.float32)
    attention = total.astype(jnp.bfloat16).astype(jnp.float32)
    out_ref[...] = (res_ref[...] + attention).astype(jnp.bfloat16)


def padded(x):
    return jnp.concatenate([x] * max(1, LANES // x.shape[0]), axis=0)


def add_block(n, k, mid_ref, gain_ref, wg_ref, wu_ref, before, after):
    gate_ref, up_ref, square_ref = after
    tokens, cols = mid_ref.shape
    experts, _, width = wg_ref.shape
    rows = tokens // n
    start = pl.multiple_of((lax.axis_index("expert") ^ k) * cols, LANES)
    got = mid_ref[...].astype(jnp.float32)
    block = jnp.concatenate([got[(i ^ k) * rows : (i ^ k) * rows + rows] for i in range(n)], axis=0)
    square = jnp.sum(block * block, axis=-1, keepdims=True)
    square_ref[...] = square + before[2][...] if before else jnp.broadcast_to(square, square_ref.shape)
    left = padded((block * gain_ref[:, pl.ds(start, cols)]).astype(jnp.bfloat16))
    for e in range(experts):
        at = slice(e * width, (e + 1) * width)
        gate = dot(left, wg_ref[e, pl.ds(start, cols)])[:tokens]
        up = dot(left, wu_ref[e, pl.ds(start, cols)])[:tokens]
        gate_ref[:, at] = gate + before[0][:, at] if before else gate
        up_ref[:, at] = up + before[1][:, at] if before else up


def part_kernel(n, k, gain_ref, wg_ref, wu_ref, _, mid_ref, *refs):
    add_block(n, k, mid_ref, gain_ref, wg_ref, wu_ref, refs[:-3], refs[-3:])


def rest_kernel(n, rest, gain_ref, wg_ref, wu_ref, wd_ref, table_ref, *refs):
    mids, sums, refs = refs[:n], refs[n : n + 3], refs[n + 3 :]
    total_ref, outs = refs[0], refs[1:n]
    gate_ref, up_ref, square_ref, sum_ref = refs[n:]
    tokens, cols = mids[0].shape
    experts, width, _ = wd_ref.shape
    rows = tokens // n
    me = lax.axis_index("expert")
    for k in rest:
        add_block(n, k, mids[k], gain_ref, wg_ref, wu_ref, sums, (gate_ref, up_ref, square_ref))
        sums = (gate_ref, up_ref, square_ref)
    inverse = lax.rsqrt(square_ref[:, :1] / (n * cols) + 1e-06)
    lane = lax.broadcasted_iota(jnp.int32, (tokens, LANES), 1) % (LANES // 2)
    for e in range(experts):
        at = slice(e * width, (e + 1) * width)
        gate = gate_ref[:, at] * inverse
        up = up_ref[:, at] * inverse
        weight = jnp.sum(
            jnp.where(lane == me * experts + e, table_ref[...], 0.0), axis=1, keepdims=True
        )
        hidden = gate / (1.0 + jnp.exp(-gate)) * up * weight
        hidden = jnp.where(weight != 0.0, hidden, 0.0).astype(jnp.bfloat16)
        down = dot(padded(hidden), wd_ref[e])[:tokens]
        if e == 0:
            sum_ref[...] = down
        else:
            sum_ref[...] += down
    total_ref[...] = sum_ref[:rows]
    for k in range(1, n):
        outs[k - 1][...] = sum_ref[k * rows : (k + 1) * rows].astype(jnp.bfloat16)


def last_kernel(n, a_ref, b_ref, *refs):
    mids, (own_ref, out_ref) = refs[:n], refs[n:]
    add_kernel(a_ref, b_ref, out_ref)
    tokens, cols = mids[0].shape
    rows = tokens // n
    me = lax.axis_index("expert")
    for k in range(n):
        got = mids[k][...].astype(jnp.float32)[k * rows : (k + 1) * rows]
        own_ref[:, pl.ds(pl.multiple_of((me ^ k) * cols, LANES), cols)] = got.astype(jnp.bfloat16)


def join_kernel(total_ref, *refs):
    *got, out_ref = refs
    total = total_ref[...]
    for ref in got:
        total = total + ref[...].astype(jnp.float32)
    out_ref[...] = total.astype(jnp.bfloat16)


def shards(
    residual,
    query_latent,
    query_rope,
    cache_latent,
    cache_rope,
    absorb_value,
    out_proj,
    norm_gain,
    routes,
    route_weights,
    w_gate,
    w_up,
    w_down,
):
    args = (
        residual,
        query_latent,
        query_rope,
        cache_latent,
        cache_rope,
        absorb_value,
        out_proj,
        norm_gain,
        routes,
        route_weights,
        w_gate,
        w_up,
        w_down,
    )
    n = lax.axis_size("expert")
    head_n = lax.axis_size("head")
    rows, model_d = residual.shape
    width, cols = out_proj.shape
    experts, _, hidden_f = w_gate.shape
    tokens = rows * n
    fits = rows == ROWS and cols % LANES == 0 and n & (n - 1) == 0 and head_n == 4
    if not fits or experts * n > LANES // 2 or width % LANES:
        return plain_shards(*args)
    scale = (absorb_value.shape[2] + query_rope.shape[2]) ** (-0.5)
    def in_vmem(x):
        return pltpu.with_memory_space_constraint(x, pltpu.VMEM)

    inputs = [
        query_latent,
        cache_latent,
        query_rope,
        cache_rope,
        absorb_value,
        residual,
        routes,
        route_weights,
        norm_gain,
    ]
    *local, gain = call(
        functools.partial(attend_kernel, scale),
        [bf16(rows, width), bf16(rows, model_d), bf16(rows, LANES), f32(1, model_d)],
        *[pltpu.with_memory_space_constraint(x, pltpu.HBM) for x in inputs],
        limit=6 << 20,
        scratch=[pltpu.VMEM(x.shape, x.dtype) for x in inputs] + [pltpu.SemaphoreType.DMA((len(inputs),))],
        specs=[pl.BlockSpec(memory_space=pltpu.HBM)] * len(inputs),
    )
    msgs = call(
        pack_kernel,
        [bf16(rows, width + cols + LANES)] * n,
        *local,
        limit=LIMIT,
        flops=FLOPS[0],
    )
    got = [swap(msgs[k], "expert", n, k) for k in range(n - 1, 0, -1)] + [msgs[0]]
    partial, res, table = call(
        project_kernel,
        [bf16(tokens, cols), f32(tokens, cols), f32(tokens, LANES)],
        in_vmem(out_proj),
        *got,
        limit=LIMIT,
        flops=FLOPS[1],
    )
    pair = call(
        add_kernel,
        bf16(tokens, cols),
        partial,
        swap(partial, "head", head_n, 1),
        limit=LIMIT,
        flops=FLOPS[2],
    )
    mid = call(
        mid_kernel,
        bf16(tokens, cols),
        pair,
        swap(pair, "head", head_n, 2),
        res,
        limit=LIMIT,
        flops=FLOPS[3],
    )
    mids = [mid] + [swap(mid, "expert", n, k) for k in range(1, n)]
    gate_weights, up_weights, down_weights = in_vmem(w_gate), in_vmem(w_up), in_vmem(w_down)
    sum_shapes = [f32(tokens, experts * hidden_f)] * 2 + [f32(tokens, LANES)]
    order = [0] + list(range(n - 1, 0, -1))
    sums = []
    for k in order[:AHEAD]:
        sums = call(
            functools.partial(part_kernel, n, k),
            sum_shapes,
            gain,
            gate_weights,
            up_weights,
            down_weights,
            mids[k],
            *sums,
            limit=LIMIT,
            flops=FLOPS[4],
        )
    own, *parts = call(
        functools.partial(rest_kernel, n, order[AHEAD:]),
        [f32(rows, model_d)] + [bf16(rows, model_d)] * (n - 1),
        gain,
        gate_weights,
        up_weights,
        down_weights,
        table,
        *mids,
        *sums,
        limit=LIMIT,
        scratch=[pltpu.VMEM(x.shape, x.dtype) for x in sum_shapes + [f32(tokens, model_d)]],
        flops=FLOPS[5],
    )
    back = [swap(parts[k - 1], "expert", n, k) for k in range(1, n)]
    mixed = call(join_kernel, bf16(rows, model_d), own, *back, limit=LIMIT)
    mixed = call(
        add_kernel,
        bf16(rows, model_d),
        mixed,
        swap(mixed, "head", head_n, 1),
        limit=LIMIT,
    )
    own_mid, mixed = call(
        functools.partial(last_kernel, n),
        [bf16(rows, model_d)] * 2,
        mixed,
        swap(mixed, "head", head_n, 2),
        *mids,
        limit=LIMIT,
    )
    return own_mid, mixed


def solution(mesh):
    in_specs = (
        P(("groups", "expert"), None),
        P(("groups", "expert"), "head", None),
        P(("groups", "expert"), "head", None),
        P(("groups", "expert"), None, None),
        P(("groups", "expert"), None, None),
        P("head", None, None),
        P("head", "expert"),
        P(),
        P(("groups", "expert"), None),
        P(("groups", "expert"), None),
        P("expert", None, "head"),
        P("expert", None, "head"),
        P("expert", "head", None),
    )
    out_specs = (P(("groups", "expert"), None), P(("groups", "expert"), None))
    return jax.shard_map(shards, mesh=mesh, in_specs=in_specs, out_specs=out_specs, check_vma=False)
```

```python
import functools

import jax
import jax.numpy as jnp
from jax import lax
from jax.experimental import pallas as pl
from jax.experimental.pallas import tpu as pltpu
from jax.sharding import PartitionSpec as P

LANES = 128
LIMIT = 4 << 20
AHEAD = 3
ROWS = 8
VMEM = pl.BlockSpec(memory_space=pltpu.VMEM)
FLOPS = (16 * 10**10, 1, 1, 1, 10**9, 10**9)


def swap(x, axis, size, step):
    return lax.ppermute(x, axis, [(s, s ^ step) for s in range(size)])


def gather_rows(x, axis):
    size = lax.axis_size(axis)
    me = lax.axis_index(axis)
    out = jnp.zeros((size,) + x.shape, x.dtype)
    out = lax.dynamic_update_index_in_dim(out, x, me, 0)
    for step in range(1, size):
        out = lax.dynamic_update_index_in_dim(out, swap(x, axis, size, step), me ^ step, 0)
    return out


def scatter_sum(blocks, axis):
    size = lax.axis_size(axis)
    me = lax.axis_index(axis)
    total = lax.dynamic_index_in_dim(blocks, me, 0, keepdims=False)
    for step in range(1, size):
        block = lax.dynamic_index_in_dim(blocks, me ^ step, 0, keepdims=False)
        total = total + swap(block.astype(jnp.bfloat16), axis, size, step).astype(jnp.float32)
    return total


def sum_all(x, axis):
    size = lax.axis_size(axis)
    step = 1
    while step < size:
        x = x + swap(x.astype(jnp.bfloat16), axis, size, step).astype(jnp.float32)
        step *= 2
    return x


def attend(query_lat, query_rot, cache_lat, cache_rot, absorb_value, score_scale):
    scores = jnp.einsum("thl,tcl->thc", query_lat, cache_lat, preferred_element_type=jnp.float32)
    scores = scores + jnp.einsum(
        "thr,tcr->thc", query_rot, cache_rot, preferred_element_type=jnp.float32
    )
    probs = jax.nn.softmax(scores * score_scale, axis=-1).astype(jnp.bfloat16)
    latent = jnp.einsum(
        "thc,tcl->thl", probs, cache_lat, preferred_element_type=jnp.float32
    ).astype(jnp.bfloat16)
    per_head = jnp.einsum(
        "thl,hlv->thv", latent, absorb_value, preferred_element_type=jnp.float32
    ).astype(jnp.bfloat16)
    return per_head.reshape(per_head.shape[0], per_head.shape[1] * per_head.shape[2])


def plain_shards(
    residual,
    query_latent,
    query_rope,
    cache_latent,
    cache_rope,
    absorb_value,
    out_proj,
    norm_gain,
    routes,
    route_weights,
    w_gate,
    w_up,
    w_down,
):
    sources = lax.axis_size("expert")
    me = lax.axis_index("expert")
    experts, model_d, hidden_f = w_gate.shape
    rows = residual.shape[0]
    tokens = rows * sources
    score_scale = (absorb_value.shape[2] + query_rope.shape[2]) ** (-0.5)
    all_res = gather_rows(residual, "expert").reshape(tokens, model_d)
    all_routes = gather_rows(routes, "expert").reshape(tokens, -1)
    all_weights = gather_rows(route_weights, "expert").reshape(tokens, -1)
    own_ids = me * experts + jnp.arange(experts, dtype=jnp.int32)
    named = all_routes[:, None, :] == own_ids[None, :, None]
    chosen = jnp.any(named, axis=2)
    weight = jnp.sum(jnp.where(named, all_weights[:, None, :], 0.0), axis=2)

    per_head = attend(
        query_latent, query_rope, cache_latent, cache_rope, absorb_value, score_scale
    )
    all_heads = gather_rows(per_head, "expert").reshape(tokens, -1)
    partial = jnp.dot(all_heads, out_proj, preferred_element_type=jnp.float32)
    summed = sum_all(partial, "head").astype(jnp.bfloat16)
    attention = gather_rows(summed, "expert")
    attention = attention.transpose(1, 0, 2).reshape(tokens, model_d)
    mid = (all_res.astype(jnp.float32) + attention.astype(jnp.float32)).astype(jnp.bfloat16)
    mid_float = mid.astype(jnp.float32)
    normed = (
        mid_float
        * lax.rsqrt(jnp.mean(mid_float * mid_float, axis=-1, keepdims=True) + 1e-06)
        * norm_gain
    ).astype(jnp.bfloat16)
    gate = jnp.einsum("td,edf->etf", normed, w_gate, preferred_element_type=jnp.float32)
    up = jnp.einsum("td,edf->etf", normed, w_up, preferred_element_type=jnp.float32)
    hidden = jnp.where(
        chosen.T[:, :, None], jax.nn.silu(gate) * up * weight.T[:, :, None], 0.0
    ).astype(jnp.bfloat16)
    down = jnp.einsum("etf,efd->td", hidden, w_down, preferred_element_type=jnp.float32)
    mixed = scatter_sum(down.reshape(sources, rows, model_d), "expert")
    mixed = sum_all(mixed, "head").astype(jnp.bfloat16)
    own_mid = lax.dynamic_slice_in_dim(mid, me * rows, rows, 0)
    return own_mid, mixed


def call(body, outs, *args, limit, scratch=(), flops=None, specs=None):
    estimate = None
    if flops is not None:
        estimate = pl.CostEstimate(flops=flops, bytes_accessed=1 << 20, transcendentals=0)
    return pl.pallas_call(
        body,
        out_shape=outs,
        in_specs=[VMEM] * len(args) if specs is None else specs,
        out_specs=jax.tree.map(lambda _: VMEM, outs),
        scratch_shapes=list(scratch),
        compiler_params=pltpu.CompilerParams(vmem_limit_bytes=limit),
        cost_estimate=estimate,
    )(*args)


def bf16(*shape):
    return jax.ShapeDtypeStruct(shape, jnp.bfloat16)


def f32(*shape):
    return jax.ShapeDtypeStruct(shape, jnp.float32)


def dot(a, b):
    return jnp.dot(a, b, preferred_element_type=jnp.float32)


def dot_t(a, b):
    return lax.dot_general(a, b, (((1,), (1,)), ((), ())), preferred_element_type=jnp.float32)


def rows_of(x, first, second):
    return x.astype(jnp.float32).reshape(first * second, x.shape[2]).astype(x.dtype)


def attend_kernel(scale, *refs):
    sources, outs, held, sems = refs[:9], refs[9:13], refs[13:22], refs[22]
    heads_ref, res_out_ref, table_ref, gain_out_ref = outs
    copies = [
        pltpu.make_async_copy(source, place, sems.at[i])
        for i, (source, place) in enumerate(zip(sources, held))
    ]
    for copy in copies:
        copy.start()
    ql_ref, cl_ref, qr_ref, cr_ref, av_ref, res_ref, routes_ref, weights_ref, gain_ref = held
    t, h, _ = ql_ref.shape
    c = cl_ref.shape[1]
    vdim = av_ref.shape[2]
    for copy in copies[:4]:
        copy.wait()
    cache = rows_of(cl_ref[...], t, c)
    scores = dot_t(rows_of(ql_ref[...], t, h), cache)
    scores = scores + dot_t(rows_of(qr_ref[...], t, h), rows_of(cr_ref[...], t, c))
    row_t = lax.broadcasted_iota(jnp.int32, (t * h, t * c), 0) // h
    col_t = lax.broadcasted_iota(jnp.int32, (t * h, t * c), 1) // c
    scores = jnp.where(row_t == col_t, scores * scale, -jnp.inf)
    top = jnp.max(scores, axis=-1, keepdims=True)
    exps = jnp.exp(scores - top)
    probs = (exps / jnp.sum(exps, axis=-1, keepdims=True)).astype(jnp.bfloat16)
    latent = dot(probs, cache).astype(jnp.bfloat16)
    to_row = lax.broadcasted_iota(jnp.int32, (t * h, t * h), 0)
    from_row = lax.broadcasted_iota(jnp.int32, (t * h, t * h), 1)
    order = (to_row // t == from_row % h) & (to_row % t == from_row // h)
    by_head = dot(jnp.where(order, 1.0, 0.0).astype(jnp.bfloat16), latent)
    for copy in copies[4:]:
        copy.wait()
    for i in range(h):
        out = dot(by_head[i * t : (i + 1) * t].astype(jnp.bfloat16), av_ref[i])
        heads_ref[:, i * vdim : (i + 1) * vdim] = out.astype(jnp.bfloat16)
    res_out_ref[...] = res_ref[...]
    gain_out_ref[...] = gain_ref[...].reshape(gain_out_ref.shape)
    lane = lax.broadcasted_iota(jnp.int32, (t, LANES), 1)
    table = jnp.zeros((t, LANES), jnp.float32)
    for k in range(routes_ref.shape[1]):
        named = lane == routes_ref[:, k : k + 1]
        table = jnp.where(named, weights_ref[:, k : k + 1], table)
    high = table.astype(jnp.bfloat16).astype(jnp.float32)
    low = pltpu.roll(table - high, LANES // 2, 1)
    table_ref[...] = jnp.where(lane < LANES // 2, high, low).astype(jnp.bfloat16)


def pack_kernel(heads_ref, res_ref, table_ref, *msgs):
    cols = res_ref.shape[1] // len(msgs)
    width = heads_ref.shape[1]
    me = lax.axis_index("expert")
    for step, msg in enumerate(msgs):
        start = pl.multiple_of((me ^ step) * cols, LANES)
        msg[:, :width] = heads_ref[...]
        msg[:, width : width + cols] = res_ref[:, pl.ds(start, cols)]
        msg[:, width + cols :] = table_ref[...]


def stacked(refs, first, last):
    blocks = [ref[:, first:last].astype(jnp.float32) for ref in refs]
    return jnp.concatenate(blocks, axis=0)


def project_kernel(proj_ref, *refs):
    *msgs, out_ref, res_ref, table_ref = refs
    msgs = msgs[::-1]
    width = proj_ref.shape[0]
    cols = proj_ref.shape[1]
    heads = stacked(msgs, 0, width).astype(jnp.bfloat16)
    out_ref[...] = dot(heads, proj_ref[...]).astype(jnp.bfloat16)
    res_ref[...] = stacked(msgs, width, width + cols)
    table_ref[...] = stacked(msgs, width + cols, width + cols + LANES)


def add_kernel(a_ref, b_ref, out_ref):
    total = a_ref[...].astype(jnp.float32) + b_ref[...].astype(jnp.float32)
    out_ref[...] = total.astype(out_ref.dtype)


def mid_kernel(a_ref, b_ref, res_ref, out_ref):
    total = a_ref[...].astype(jnp.float32) + b_ref[...].astype(jnp.float32)
    attention = total.astype(jnp.bfloat16).astype(jnp.float32)
    out_ref[...] = (res_ref[...] + attention).astype(jnp.bfloat16)


def padded(x):
    return jnp.concatenate([x] * max(1, LANES // x.shape[0]), axis=0)


def add_block(n, k, mid_ref, gain_ref, wg_ref, wu_ref, before, after):
    gate_ref, up_ref, square_ref = after
    tokens, cols = mid_ref.shape
    experts, _, width = wg_ref.shape
    rows = tokens // n
    start = pl.multiple_of((lax.axis_index("expert") ^ k) * cols, LANES)
    got = mid_ref[...].astype(jnp.float32)
    block = jnp.concatenate([got[(i ^ k) * rows : (i ^ k) * rows + rows] for i in range(n)], axis=0)
    square = jnp.sum(block * block, axis=-1, keepdims=True)
    square_ref[...] = square + before[2][...] if before else jnp.broadcast_to(square, square_ref.shape)
    left = padded((block * gain_ref[:, pl.ds(start, cols)]).astype(jnp.bfloat16))
    for e in range(experts):
        at = slice(e * width, (e + 1) * width)
        gate = dot(left, wg_ref[e, pl.ds(start, cols)])[:tokens]
        up = dot(left, wu_ref[e, pl.ds(start, cols)])[:tokens]
        gate_ref[:, at] = gate + before[0][:, at] if before else gate
        up_ref[:, at] = up + before[1][:, at] if before else up


def part_kernel(n, k, gain_ref, wg_ref, wu_ref, _, mid_ref, *refs):
    add_block(n, k, mid_ref, gain_ref, wg_ref, wu_ref, refs[:-3], refs[-3:])


def rest_kernel(n, rest, gain_ref, wg_ref, wu_ref, wd_ref, table_ref, *refs):
    mids, sums, refs = refs[:n], refs[n : n + 3], refs[n + 3 :]
    total_ref, outs = refs[0], refs[1:n]
    gate_ref, up_ref, square_ref, sum_ref = refs[n:]
    tokens, cols = mids[0].shape
    experts, width, _ = wd_ref.shape
    rows = tokens // n
    me = lax.axis_index("expert")
    for k in rest:
        add_block(n, k, mids[k], gain_ref, wg_ref, wu_ref, sums, (gate_ref, up_ref, square_ref))
        sums = (gate_ref, up_ref, square_ref)
    inverse = lax.rsqrt(square_ref[:, :1] / (n * cols) + 1e-06)
    lane = lax.broadcasted_iota(jnp.int32, (tokens, LANES), 1) % (LANES // 2)
    for e in range(experts):
        at = slice(e * width, (e + 1) * width)
        gate = gate_ref[:, at] * inverse
        up = up_ref[:, at] * inverse
        weight = jnp.sum(
            jnp.where(lane == me * experts + e, table_ref[...], 0.0), axis=1, keepdims=True
        )
        hidden = gate / (1.0 + jnp.exp(-gate)) * up * weight
        hidden = jnp.where(weight != 0.0, hidden, 0.0).astype(jnp.bfloat16)
        down = dot(padded(hidden), wd_ref[e])[:tokens]
        if e == 0:
            sum_ref[...] = down
        else:
            sum_ref[...] += down
    total_ref[...] = sum_ref[:rows]
    for k in range(1, n):
        outs[k - 1][...] = sum_ref[k * rows : (k + 1) * rows].astype(jnp.bfloat16)


def last_kernel(n, a_ref, b_ref, *refs):
    mids, (own_ref, out_ref) = refs[:n], refs[n:]
    add_kernel(a_ref, b_ref, out_ref)
    tokens, cols = mids[0].shape
    rows = tokens // n
    me = lax.axis_index("expert")
    for k in range(n):
        got = mids[k][...].astype(jnp.float32)[k * rows : (k + 1) * rows]
        own_ref[:, pl.ds(pl.multiple_of((me ^ k) * cols, LANES), cols)] = got.astype(jnp.bfloat16)


def join_kernel(total_ref, *refs):
    *got, out_ref = refs
    total = total_ref[...]
    for ref in got:
        total = total + ref[...].astype(jnp.float32)
    out_ref[...] = total.astype(jnp.bfloat16)


def shards(
    residual,
    query_latent,
    query_rope,
    cache_latent,
    cache_rope,
    absorb_value,
    out_proj,
    norm_gain,
    routes,
    route_weights,
    w_gate,
    w_up,
    w_down,
):
    args = (
        residual,
        query_latent,
        query_rope,
        cache_latent,
        cache_rope,
        absorb_value,
        out_proj,
        norm_gain,
        routes,
        route_weights,
        w_gate,
        w_up,
        w_down,
    )
    n = lax.axis_size("expert")
    head_n = lax.axis_size("head")
    rows, model_d = residual.shape
    width, cols = out_proj.shape
    experts, _, hidden_f = w_gate.shape
    tokens = rows * n
    fits = rows == ROWS and cols % LANES == 0 and n & (n - 1) == 0 and head_n == 4
    if not fits or experts * n > LANES // 2 or width % LANES:
        return plain_shards(*args)
    scale = (absorb_value.shape[2] + query_rope.shape[2]) ** (-0.5)
    def in_vmem(x):
        return pltpu.with_memory_space_constraint(x, pltpu.VMEM)

    inputs = [
        query_latent,
        cache_latent,
        query_rope,
        cache_rope,
        absorb_value,
        residual,
        routes,
        route_weights,
        norm_gain,
    ]
    *local, gain = call(
        functools.partial(attend_kernel, scale),
        [bf16(rows, width), bf16(rows, model_d), bf16(rows, LANES), f32(1, model_d)],
        *[pltpu.with_memory_space_constraint(x, pltpu.HBM) for x in inputs],
        limit=6 << 20,
        scratch=[pltpu.VMEM(x.shape, x.dtype) for x in inputs] + [pltpu.SemaphoreType.DMA((len(inputs),))],
        specs=[pl.BlockSpec(memory_space=pltpu.HBM)] * len(inputs),
    )
    msgs = call(
        pack_kernel,
        [bf16(rows, width + cols + LANES)] * n,
        *local,
        limit=LIMIT,
        flops=FLOPS[0],
    )
    got = [swap(msgs[k], "expert", n, k) for k in range(n - 1, 0, -1)] + [msgs[0]]
    partial, res, table = call(
        project_kernel,
        [bf16(tokens, cols), f32(tokens, cols), f32(tokens, LANES)],
        in_vmem(out_proj),
        *got,
        limit=LIMIT,
        flops=FLOPS[1],
    )
    pair = call(
        add_kernel,
        bf16(tokens, cols),
        partial,
        swap(partial, "head", head_n, 1),
        limit=LIMIT,
        flops=FLOPS[2],
    )
    mid = call(
        mid_kernel,
        bf16(tokens, cols),
        pair,
        swap(pair, "head", head_n, 2),
        res,
        limit=LIMIT,
        flops=FLOPS[3],
    )
    mids = [mid] + [swap(mid, "expert", n, k) for k in range(1, n)]
    gate_weights, up_weights, down_weights = in_vmem(w_gate), in_vmem(w_up), in_vmem(w_down)
    sum_shapes = [f32(tokens, experts * hidden_f)] * 2 + [f32(tokens, LANES)]
    order = list(range(n))
    sums = []
    for k in order[:AHEAD]:
        sums = call(
            functools.partial(part_kernel, n, k),
            sum_shapes,
            gain,
            gate_weights,
            up_weights,
            down_weights,
            mids[k],
            *sums,
            limit=LIMIT,
            flops=FLOPS[4],
        )
    own, *parts = call(
        functools.partial(rest_kernel, n, order[AHEAD:]),
        [f32(rows, model_d)] + [bf16(rows, model_d)] * (n - 1),
        gain,
        gate_weights,
        up_weights,
        down_weights,
        table,
        *mids,
        *sums,
        limit=LIMIT,
        scratch=[pltpu.VMEM(x.shape, x.dtype) for x in sum_shapes + [f32(tokens, model_d)]],
        flops=FLOPS[5],
    )
    back = [swap(parts[k - 1], "expert", n, k) for k in range(1, n)]
    mixed = call(join_kernel, bf16(rows, model_d), own, *back, limit=LIMIT)
    mixed = call(
        add_kernel,
        bf16(rows, model_d),
        mixed,
        swap(mixed, "head", head_n, 1),
        limit=LIMIT,
    )
    own_mid, mixed = call(
        functools.partial(last_kernel, n),
        [bf16(rows, model_d)] * 2,
        mixed,
        swap(mixed, "head", head_n, 2),
        *mids,
        limit=LIMIT,
    )
    return own_mid, mixed


def solution(mesh):
    in_specs = (
        P(("groups", "expert"), None),
        P(("groups", "expert"), "head", None),
        P(("groups", "expert"), "head", None),
        P(("groups", "expert"), None, None),
        P(("groups", "expert"), None, None),
        P("head", None, None),
        P("head", "expert"),
        P(),
        P(("groups", "expert"), None),
        P(("groups", "expert"), None),
        P("expert", None, "head"),
        P("expert", None, "head"),
        P("expert", "head", None),
    )
    out_specs = (P(("groups", "expert"), None), P(("groups", "expert"), None))
    return jax.shard_map(shards, mesh=mesh, in_specs=in_specs, out_specs=out_specs, check_vma=False)
```

```python
import functools

import jax
import jax.numpy as jnp
from jax import lax
from jax.experimental import pallas as pl
from jax.experimental.pallas import tpu as pltpu
from jax.sharding import PartitionSpec as P

LANES = 128
LIMIT = 4 << 20
AHEAD = 3
ROWS = 8
VMEM = pl.BlockSpec(memory_space=pltpu.VMEM)
FLOPS = (16 * 10**10, 1, 1, 1, 10**9, 10**9)


def swap(x, axis, size, step):
    return lax.ppermute(x, axis, [(s, s ^ step) for s in range(size)])


def gather_rows(x, axis):
    size = lax.axis_size(axis)
    me = lax.axis_index(axis)
    out = jnp.zeros((size,) + x.shape, x.dtype)
    out = lax.dynamic_update_index_in_dim(out, x, me, 0)
    for step in range(1, size):
        out = lax.dynamic_update_index_in_dim(out, swap(x, axis, size, step), me ^ step, 0)
    return out


def scatter_sum(blocks, axis):
    size = lax.axis_size(axis)
    me = lax.axis_index(axis)
    total = lax.dynamic_index_in_dim(blocks, me, 0, keepdims=False)
    for step in range(1, size):
        block = lax.dynamic_index_in_dim(blocks, me ^ step, 0, keepdims=False)
        total = total + swap(block.astype(jnp.bfloat16), axis, size, step).astype(jnp.float32)
    return total


def sum_all(x, axis):
    size = lax.axis_size(axis)
    step = 1
    while step < size:
        x = x + swap(x.astype(jnp.bfloat16), axis, size, step).astype(jnp.float32)
        step *= 2
    return x


def attend(query_lat, query_rot, cache_lat, cache_rot, absorb_value, score_scale):
    scores = jnp.einsum("thl,tcl->thc", query_lat, cache_lat, preferred_element_type=jnp.float32)
    scores = scores + jnp.einsum(
        "thr,tcr->thc", query_rot, cache_rot, preferred_element_type=jnp.float32
    )
    probs = jax.nn.softmax(scores * score_scale, axis=-1).astype(jnp.bfloat16)
    latent = jnp.einsum(
        "thc,tcl->thl", probs, cache_lat, preferred_element_type=jnp.float32
    ).astype(jnp.bfloat16)
    per_head = jnp.einsum(
        "thl,hlv->thv", latent, absorb_value, preferred_element_type=jnp.float32
    ).astype(jnp.bfloat16)
    return per_head.reshape(per_head.shape[0], per_head.shape[1] * per_head.shape[2])


def plain_shards(
    residual,
    query_latent,
    query_rope,
    cache_latent,
    cache_rope,
    absorb_value,
    out_proj,
    norm_gain,
    routes,
    route_weights,
    w_gate,
    w_up,
    w_down,
):
    sources = lax.axis_size("expert")
    me = lax.axis_index("expert")
    experts, model_d, hidden_f = w_gate.shape
    rows = residual.shape[0]
    tokens = rows * sources
    score_scale = (absorb_value.shape[2] + query_rope.shape[2]) ** (-0.5)
    all_res = gather_rows(residual, "expert").reshape(tokens, model_d)
    all_routes = gather_rows(routes, "expert").reshape(tokens, -1)
    all_weights = gather_rows(route_weights, "expert").reshape(tokens, -1)
    own_ids = me * experts + jnp.arange(experts, dtype=jnp.int32)
    named = all_routes[:, None, :] == own_ids[None, :, None]
    chosen = jnp.any(named, axis=2)
    weight = jnp.sum(jnp.where(named, all_weights[:, None, :], 0.0), axis=2)

    per_head = attend(
        query_latent, query_rope, cache_latent, cache_rope, absorb_value, score_scale
    )
    all_heads = gather_rows(per_head, "expert").reshape(tokens, -1)
    partial = jnp.dot(all_heads, out_proj, preferred_element_type=jnp.float32)
    summed = sum_all(partial, "head").astype(jnp.bfloat16)
    attention = gather_rows(summed, "expert")
    attention = attention.transpose(1, 0, 2).reshape(tokens, model_d)
    mid = (all_res.astype(jnp.float32) + attention.astype(jnp.float32)).astype(jnp.bfloat16)
    mid_float = mid.astype(jnp.float32)
    normed = (
        mid_float
        * lax.rsqrt(jnp.mean(mid_float * mid_float, axis=-1, keepdims=True) + 1e-06)
        * norm_gain
    ).astype(jnp.bfloat16)
    gate = jnp.einsum("td,edf->etf", normed, w_gate, preferred_element_type=jnp.float32)
    up = jnp.einsum("td,edf->etf", normed, w_up, preferred_element_type=jnp.float32)
    hidden = jnp.where(
        chosen.T[:, :, None], jax.nn.silu(gate) * up * weight.T[:, :, None], 0.0
    ).astype(jnp.bfloat16)
    down = jnp.einsum("etf,efd->td", hidden, w_down, preferred_element_type=jnp.float32)
    mixed = scatter_sum(down.reshape(sources, rows, model_d), "expert")
    mixed = sum_all(mixed, "head").astype(jnp.bfloat16)
    own_mid = lax.dynamic_slice_in_dim(mid, me * rows, rows, 0)
    return own_mid, mixed


def call(body, outs, *args, limit, scratch=(), flops=None, specs=None):
    estimate = None
    if flops is not None:
        estimate = pl.CostEstimate(flops=flops, bytes_accessed=1 << 20, transcendentals=0)
    return pl.pallas_call(
        body,
        out_shape=outs,
        in_specs=[VMEM] * len(args) if specs is None else specs,
        out_specs=jax.tree.map(lambda _: VMEM, outs),
        scratch_shapes=list(scratch),
        compiler_params=pltpu.CompilerParams(vmem_limit_bytes=limit),
        cost_estimate=estimate,
    )(*args)


def bf16(*shape):
    return jax.ShapeDtypeStruct(shape, jnp.bfloat16)


def f32(*shape):
    return jax.ShapeDtypeStruct(shape, jnp.float32)


def dot(a, b):
    return jnp.dot(a, b, preferred_element_type=jnp.float32)


def dot_t(a, b):
    return lax.dot_general(a, b, (((1,), (1,)), ((), ())), preferred_element_type=jnp.float32)


def rows_of(x, first, second):
    return x.astype(jnp.float32).reshape(first * second, x.shape[2]).astype(x.dtype)


def attend_kernel(scale, *refs):
    sources, outs, held, sems = refs[:9], refs[9:13], refs[13:22], refs[22]
    heads_ref, res_out_ref, table_ref, gain_out_ref = outs
    copies = [
        pltpu.make_async_copy(source, place, sems.at[i])
        for i, (source, place) in enumerate(zip(sources, held))
    ]
    for copy in copies:
        copy.start()
    ql_ref, cl_ref, qr_ref, cr_ref, av_ref, res_ref, routes_ref, weights_ref, gain_ref = held
    t, h, _ = ql_ref.shape
    c = cl_ref.shape[1]
    vdim = av_ref.shape[2]
    for copy in copies[:4]:
        copy.wait()
    cache = rows_of(cl_ref[...], t, c)
    scores = dot_t(rows_of(ql_ref[...], t, h), cache)
    scores = scores + dot_t(rows_of(qr_ref[...], t, h), rows_of(cr_ref[...], t, c))
    row_t = lax.broadcasted_iota(jnp.int32, (t * h, t * c), 0) // h
    col_t = lax.broadcasted_iota(jnp.int32, (t * h, t * c), 1) // c
    scores = jnp.where(row_t == col_t, scores * scale, -jnp.inf)
    top = jnp.max(scores, axis=-1, keepdims=True)
    exps = jnp.exp(scores - top)
    probs = (exps / jnp.sum(exps, axis=-1, keepdims=True)).astype(jnp.bfloat16)
    latent = dot(probs, cache).astype(jnp.bfloat16)
    to_row = lax.broadcasted_iota(jnp.int32, (t * h, t * h), 0)
    from_row = lax.broadcasted_iota(jnp.int32, (t * h, t * h), 1)
    order = (to_row // t == from_row % h) & (to_row % t == from_row // h)
    by_head = dot(jnp.where(order, 1.0, 0.0).astype(jnp.bfloat16), latent)
    for copy in copies[4:]:
        copy.wait()
    for i in range(h):
        out = dot(by_head[i * t : (i + 1) * t].astype(jnp.bfloat16), av_ref[i])
        heads_ref[:, i * vdim : (i + 1) * vdim] = out.astype(jnp.bfloat16)
    res_out_ref[...] = res_ref[...]
    gain_out_ref[...] = gain_ref[...].reshape(gain_out_ref.shape)
    lane = lax.broadcasted_iota(jnp.int32, (t, LANES), 1)
    table = jnp.zeros((t, LANES), jnp.float32)
    for k in range(routes_ref.shape[1]):
        named = lane == routes_ref[:, k : k + 1]
        table = jnp.where(named, weights_ref[:, k : k + 1], table)
    high = table.astype(jnp.bfloat16).astype(jnp.float32)
    low = pltpu.roll(table - high, LANES // 2, 1)
    table_ref[...] = jnp.where(lane < LANES // 2, high, low).astype(jnp.bfloat16)


def pack_kernel(heads_ref, res_ref, table_ref, *msgs):
    cols = res_ref.shape[1] // len(msgs)
    width = heads_ref.shape[1]
    me = lax.axis_index("expert")
    for step, msg in enumerate(msgs):
        start = pl.multiple_of((me ^ step) * cols, LANES)
        msg[:, :width] = heads_ref[...]
        msg[:, width : width + cols] = res_ref[:, pl.ds(start, cols)]
        msg[:, width + cols :] = table_ref[...]


def stacked(refs, first, last):
    blocks = [ref[:, first:last].astype(jnp.float32) for ref in refs]
    return jnp.concatenate(blocks, axis=0)


def project_kernel(proj_ref, *refs):
    *msgs, out_ref, res_ref, table_ref = refs
    msgs = msgs[::-1]
    width = proj_ref.shape[0]
    cols = proj_ref.shape[1]
    heads = stacked(msgs, 0, width).astype(jnp.bfloat16)
    out_ref[...] = dot(heads, proj_ref[...]).astype(jnp.bfloat16)
    res_ref[...] = stacked(msgs, width, width + cols)
    table_ref[...] = stacked(msgs, width + cols, width + cols + LANES)


def add_kernel(a_ref, b_ref, out_ref):
    total = a_ref[...].astype(jnp.float32) + b_ref[...].astype(jnp.float32)
    out_ref[...] = total.astype(out_ref.dtype)


def mid_kernel(a_ref, b_ref, res_ref, out_ref):
    total = a_ref[...].astype(jnp.float32) + b_ref[...].astype(jnp.float32)
    attention = total.astype(jnp.bfloat16).astype(jnp.float32)
    out_ref[...] = (res_ref[...] + attention).astype(jnp.bfloat16)


def padded(x):
    return jnp.concatenate([x] * max(1, LANES // x.shape[0]), axis=0)


def add_block(n, k, mid_ref, gain_ref, wg_ref, wu_ref, before, after):
    gate_ref, up_ref, square_ref = after
    tokens, cols = mid_ref.shape
    experts, _, width = wg_ref.shape
    rows = tokens // n
    start = pl.multiple_of((lax.axis_index("expert") ^ k) * cols, LANES)
    got = mid_ref[...].astype(jnp.float32)
    block = jnp.concatenate([got[(i ^ k) * rows : (i ^ k) * rows + rows] for i in range(n)], axis=0)
    square = jnp.sum(block * block, axis=-1, keepdims=True)
    square_ref[...] = square + before[2][...] if before else jnp.broadcast_to(square, square_ref.shape)
    left = padded((block * gain_ref[:, pl.ds(start, cols)]).astype(jnp.bfloat16))
    for e in range(experts):
        at = slice(e * width, (e + 1) * width)
        gate = dot(left, wg_ref[e, pl.ds(start, cols)])[:tokens]
        up = dot(left, wu_ref[e, pl.ds(start, cols)])[:tokens]
        gate_ref[:, at] = gate + before[0][:, at] if before else gate
        up_ref[:, at] = up + before[1][:, at] if before else up


def part_kernel(n, k, gain_ref, wg_ref, wu_ref, _, mid_ref, *refs):
    add_block(n, k, mid_ref, gain_ref, wg_ref, wu_ref, refs[:-3], refs[-3:])


def rest_kernel(n, rest, gain_ref, wg_ref, wu_ref, wd_ref, table_ref, *refs):
    mids, sums, refs = refs[:n], refs[n : n + 3], refs[n + 3 :]
    total_ref, outs = refs[0], refs[1:n]
    gate_ref, up_ref, square_ref, sum_ref = refs[n:]
    tokens, cols = mids[0].shape
    experts, width, _ = wd_ref.shape
    rows = tokens // n
    me = lax.axis_index("expert")
    for k in rest:
        add_block(n, k, mids[k], gain_ref, wg_ref, wu_ref, sums, (gate_ref, up_ref, square_ref))
        sums = (gate_ref, up_ref, square_ref)
    inverse = lax.rsqrt(square_ref[:, :1] / (n * cols) + 1e-06)
    lane = lax.broadcasted_iota(jnp.int32, (tokens, LANES), 1) % (LANES // 2)
    for e in range(experts):
        at = slice(e * width, (e + 1) * width)
        gate = gate_ref[:, at] * inverse
        up = up_ref[:, at] * inverse
        weight = jnp.sum(
            jnp.where(lane == me * experts + e, table_ref[...], 0.0), axis=1, keepdims=True
        )
        hidden = gate / (1.0 + jnp.exp(-gate)) * up * weight
        hidden = jnp.where(weight != 0.0, hidden, 0.0).astype(jnp.bfloat16)
        down = dot(padded(hidden), wd_ref[e])[:tokens]
        if e == 0:
            sum_ref[...] = down
        else:
            sum_ref[...] += down
    total_ref[...] = sum_ref[:rows]
    for k in range(1, n):
        outs[k - 1][...] = sum_ref[k * rows : (k + 1) * rows].astype(jnp.bfloat16)


def last_kernel(n, a_ref, b_ref, *refs):
    mids, (own_ref, out_ref) = refs[:n], refs[n:]
    add_kernel(a_ref, b_ref, out_ref)
    tokens, cols = mids[0].shape
    rows = tokens // n
    me = lax.axis_index("expert")
    for k in range(n):
        got = mids[k][...].astype(jnp.float32)[k * rows : (k + 1) * rows]
        own_ref[:, pl.ds(pl.multiple_of((me ^ k) * cols, LANES), cols)] = got.astype(jnp.bfloat16)


def join_kernel(total_ref, *refs):
    *got, out_ref = refs
    total = total_ref[...]
    for ref in got:
        total = total + ref[...].astype(jnp.float32)
    out_ref[...] = total.astype(jnp.bfloat16)


def shards(
    residual,
    query_latent,
    query_rope,
    cache_latent,
    cache_rope,
    absorb_value,
    out_proj,
    norm_gain,
    routes,
    route_weights,
    w_gate,
    w_up,
    w_down,
):
    args = (
        residual,
        query_latent,
        query_rope,
        cache_latent,
        cache_rope,
        absorb_value,
        out_proj,
        norm_gain,
        routes,
        route_weights,
        w_gate,
        w_up,
        w_down,
    )
    n = lax.axis_size("expert")
    head_n = lax.axis_size("head")
    rows, model_d = residual.shape
    width, cols = out_proj.shape
    experts, _, hidden_f = w_gate.shape
    tokens = rows * n
    fits = rows == ROWS and cols % LANES == 0 and n & (n - 1) == 0 and head_n == 4
    if not fits or experts * n > LANES // 2 or width % LANES:
        return plain_shards(*args)
    scale = (absorb_value.shape[2] + query_rope.shape[2]) ** (-0.5)
    def in_vmem(x):
        return pltpu.with_memory_space_constraint(x, pltpu.VMEM)

    inputs = [
        query_latent,
        cache_latent,
        query_rope,
        cache_rope,
        absorb_value,
        residual,
        routes,
        route_weights,
        norm_gain,
    ]
    *local, gain = call(
        functools.partial(attend_kernel, scale),
        [bf16(rows, width), bf16(rows, model_d), bf16(rows, LANES), f32(1, model_d)],
        *[pltpu.with_memory_space_constraint(x, pltpu.HBM) for x in inputs],
        limit=6 << 20,
        scratch=[pltpu.VMEM(x.shape, x.dtype) for x in inputs] + [pltpu.SemaphoreType.DMA((len(inputs),))],
        specs=[pl.BlockSpec(memory_space=pltpu.HBM)] * len(inputs),
    )
    msgs = call(
        pack_kernel,
        [bf16(rows, width + cols + LANES)] * n,
        *local,
        limit=LIMIT,
        flops=FLOPS[0],
    )
    got = [swap(msgs[k], "expert", n, k) for k in range(n - 1, 0, -1)] + [msgs[0]]
    partial, res, table = call(
        project_kernel,
        [bf16(tokens, cols), f32(tokens, cols), f32(tokens, LANES)],
        in_vmem(out_proj),
        *got,
        limit=LIMIT,
        flops=FLOPS[1],
    )
    pair = call(
        add_kernel,
        bf16(tokens, cols),
        partial,
        swap(partial, "head", head_n, 1),
        limit=LIMIT,
        flops=FLOPS[2],
    )
    mid = call(
        mid_kernel,
        bf16(tokens, cols),
        pair,
        swap(pair, "head", head_n, 2),
        res,
        limit=LIMIT,
        flops=FLOPS[3],
    )
    mids = [mid] + [swap(mid, "expert", n, k) for k in range(1, n)]
    gate_weights, up_weights, down_weights = in_vmem(w_gate), in_vmem(w_up), in_vmem(w_down)
    sum_shapes = [f32(tokens, experts * hidden_f)] * 2 + [f32(tokens, LANES)]
    order = list(range(n))
    sums = []
    for k in order[:AHEAD]:
        sums = call(
            functools.partial(part_kernel, n, k),
            sum_shapes,
            gain,
            gate_weights,
            up_weights,
            down_weights,
            mids[k],
            *sums,
            limit=LIMIT,
            flops=FLOPS[4],
        )
    own, *parts = call(
        functools.partial(rest_kernel, n, order[AHEAD:]),
        [f32(rows, model_d)] + [bf16(rows, model_d)] * (n - 1),
        gain,
        gate_weights,
        up_weights,
        down_weights,
        table,
        *mids,
        *sums,
        limit=LIMIT,
        scratch=[pltpu.VMEM(x.shape, x.dtype) for x in sum_shapes + [f32(tokens, model_d)]],
        flops=FLOPS[5],
    )
    back = [swap(parts[k - 1], "expert", n, k) for k in range(1, n)]
    mixed = call(join_kernel, bf16(rows, model_d), own, *back, limit=LIMIT)
    mixed = call(
        add_kernel,
        bf16(rows, model_d),
        mixed,
        swap(mixed, "head", head_n, 2),
        limit=LIMIT,
    )
    own_mid, mixed = call(
        functools.partial(last_kernel, n),
        [bf16(rows, model_d)] * 2,
        mixed,
        swap(mixed, "head", head_n, 1),
        *mids,
        limit=LIMIT,
    )
    return own_mid, mixed


def solution(mesh):
    in_specs = (
        P(("groups", "expert"), None),
        P(("groups", "expert"), "head", None),
        P(("groups", "expert"), "head", None),
        P(("groups", "expert"), None, None),
        P(("groups", "expert"), None, None),
        P("head", None, None),
        P("head", "expert"),
        P(),
        P(("groups", "expert"), None),
        P(("groups", "expert"), None),
        P("expert", None, "head"),
        P("expert", None, "head"),
        P("expert", "head", None),
    )
    out_specs = (P(("groups", "expert"), None), P(("groups", "expert"), None))
    return jax.shard_map(shards, mesh=mesh, in_specs=in_specs, out_specs=out_specs, check_vma=False)
```
